32 devices in a mesh: rows: 8 (over y, x, core), bands: 4 (over z).
Axes of the slice: x: 2, y: 2, z: 4, core: 2. Of those that a mesh axis runs over, the one named last changes fastest.
Arguments:
- psi_panels: float32 [8192, 256], P('rows', 'bands'), may hold values from -6 to 6
- rotation: float32 [256, 8000], P('rows', 'bands'), may hold values from -0.375 to 0.375
- accumulated: float32 [8192, 8000], P('rows', 'bands'), may hold values from -6 to 6
Outputs:
- rotated: float32 [8192, 8000], P('rows', 'bands')
The draws below stay inside these ranges and needn't reach their ends.
All inputs are finite; a program needn't handle non-finite values.
Results may differ from the reference program's by a relative error of at most 0.000059.
Values sent between devices are 32-bit elements; how exact they have to be, the bound alone decides.
A program may use at most 64 MiB of HBM per device.

```python
import jax
import jax.numpy as jnp
from jax import lax

NB = 8000
KW = 256
MROWS = 8192


def shard_levels(key, extent, cuts, least, largest):
    def one(position, parts):
        draws = jax.random.uniform(jax.random.fold_in(jax.random.fold_in(key, 6), position), (parts,), jnp.float32, least / len(cuts), largest / len(cuts))
        return jnp.repeat(jnp.exp(draws), extent[position] // parts).reshape((-1,) + (1,) * (len(extent) - position - 1))

    loudness = one(*cuts[0])
    for cut in cuts[1:]:
        loudness = loudness * one(*cut)
    return loudness


def noise(key, shape, deviation, most, pieces=(), dtype=jnp.bfloat16):
    values = deviation * jax.random.normal(key, shape, jnp.float32)
    if pieces:
        values = values * shard_levels(key, shape, pieces, -0.22, 0.18)
    return jnp.clip(values, -most, most).astype(dtype)


def setup_inputs(seed: int = 0) -> dict:
    streams_of = jax.random.split(jax.random.key(seed), 4)
    psi_panels = noise(streams_of[0], (MROWS, KW), 1.0, 6.0, ((0, 8), (1, 4)), jnp.float32)
    rotation = noise(streams_of[1], (KW, NB), KW ** -0.5, 0.375, ((0, 8), (1, 4)), jnp.float32)
    accumulated = noise(streams_of[2], (MROWS, NB), 1.0, 6.0, ((0, 8), (1, 4)), jnp.float32)
    return dict(psi_panels=psi_panels, rotation=rotation, accumulated=accumulated)


def reference(psi_panels, rotation, accumulated):
    product = jnp.dot(psi_panels, rotation, precision=lax.Precision.HIGHEST, preferred_element_type=jnp.float32)
    return accumulated + product
```

```python
import functools

import jax
import jax.numpy as jnp
from jax import lax
from jax.experimental import pallas as pl
from jax.experimental.pallas import tpu as pltpu
from jax.sharding import PartitionSpec as P

MESH = pl.DeviceIdType.MESH
CHUNK = 256


def split(x):
    high = x.astype(jnp.bfloat16)
    low = (x - high.astype(jnp.float32)).astype(jnp.bfloat16)
    return high, low


def kernel(n_rows, n_bands, psi_ref, rot_ref, acc_ref, out_ref,
           psi_all, rot_all, rot_split,
           psi_recv, psi_send, rot_recv, peer_send, twin_send, local_sem):
    r = lax.axis_index("rows")
    z = lax.axis_index("bands")
    n_chips = n_rows // 2
    chip, core = r // 2, r % 2
    twin = 2 * chip + 1 - core
    kz, mrows = psi_ref.shape
    kr, nb = rot_ref.shape
    chunks = mrows // CHUNK

    def peer(d):
        return 2 * lax.rem(chip + d, n_chips) + core

    def columns(c):
        return pl.ds(pl.multiple_of(c * CHUNK, CHUNK), CHUNK)

    load_acc = pltpu.make_async_copy(acc_ref, out_ref, local_sem.at[0])
    load_psi = pltpu.make_async_copy(psi_ref, psi_all.at[z], local_sem.at[1])
    load_rot = pltpu.make_async_copy(rot_ref, rot_all.at[r], local_sem.at[2])

    barrier = pltpu.get_barrier_semaphore()

    def greet(rows, bands):
        pl.semaphore_signal(barrier, inc=1, device_id=(rows, bands), device_id_type=MESH)

    pl.when(z > 0)(lambda: greet(r, z - 1))
    pl.when(z < n_bands - 1)(lambda: greet(r, z + 1))
    greet(twin, z)

    @pl.loop(1, n_chips)
    def _(d):
        greet(peer(d), z)

    expected = n_chips + jnp.where(z > 0, 1, 0) + jnp.where(z < n_bands - 1, 1, 0)
    pl.semaphore_wait(barrier, expected)

    def psi_copy(source, c, way, own=False):
        here = psi_ref if own else psi_all.at[source]
        target = z + 2 * way - 1
        return pltpu.make_async_remote_copy(
            src_ref=here.at[:, columns(c)],
            dst_ref=psi_all.at[source, :, columns(c)],
            send_sem=psi_send.at[way, source, c],
            recv_sem=psi_recv.at[source, c],
            device_id=(r, target), device_id_type=MESH)

    def rot_copy(source, target, send_sem, own=False):
        return pltpu.make_async_remote_copy(
            src_ref=rot_ref if own else rot_all.at[source],
            dst_ref=rot_all.at[source],
            send_sem=send_sem, recv_sem=rot_recv.at[source],
            device_id=(target, z), device_id_type=MESH)

    @pl.loop(0, chunks)
    def _(c):
        pl.when(z > 0)(lambda: psi_copy(z, c, 0, own=True).start())
        pl.when(z < n_bands - 1)(lambda: psi_copy(z, c, 1, own=True).start())

    @pl.loop(1, n_chips)
    def _(d):
        rot_copy(r, peer(d), peer_send.at[d], own=True).start()

    rot_copy(r, twin, twin_send.at[0], own=True).start()
    load_psi.start()
    load_rot.start()
    load_acc.start()

    if n_bands > 2:
        @pl.loop(1, n_bands - 1)
        def _(h):
            @pl.loop(0, chunks)
            def _(c):
                @pl.when((z - h >= 0) & (z + 1 < n_bands))
                def _():
                    copy = psi_copy(z - h, c, 1)
                    copy.wait_recv()
                    copy.start()

                @pl.when((z + h < n_bands) & (z > 0))
                def _():
                    copy = psi_copy(z + h, c, 0)
                    copy.wait_recv()
                    copy.start()

    @pl.loop(1, n_chips)
    def _(d):
        source = peer(n_chips - d)
        copy = rot_copy(source, twin, twin_send.at[d])
        copy.wait_recv()
        copy.start()

    @pl.loop(0, n_chips)
    def _(d):
        source = 2 * lax.rem(chip + d, n_chips) + 1 - core
        rot_copy(source, twin, twin_send.at[d]).wait_recv()

    load_rot.wait()
    for start in range(0, nb, 128):
        width = min(128, nb - start)
        block = rot_all[:, :, start:start + width].reshape(n_rows * kr, width).T
        high, low = split(block)
        rot_split[start:start + width, :] = jnp.concatenate([high, low, high], axis=1)

    load_psi.wait()
    load_acc.wait()

    @pl.loop(0, chunks)
    def _(c):
        @pl.when(z == 0)
        def _():
            @pl.loop(1, n_bands)
            def _(source):
                psi_copy(source, c, 1).wait_recv()

        @pl.when(z == n_bands - 1)
        def _():
            @pl.loop(0, n_bands - 1)
            def _(source):
                psi_copy(source, c, 0).wait_recv()

        high, low = split(psi_all[:, :, columns(c)].reshape(n_bands * kz, CHUNK))
        operand = jnp.concatenate([high, high, low], axis=0)
        out_ref[:, columns(c)] += jnp.dot(
            rot_split[...], operand, preferred_element_type=jnp.float32)

    @pl.loop(0, chunks)
    def _(c):
        @pl.when(z < n_bands - 1)
        def _():
            @pl.loop(0, z + 1)
            def _(source):
                psi_copy(source, c, 1).wait_send()

        @pl.when(z > 0)
        def _():
            @pl.loop(z, n_bands)
            def _(source):
                psi_copy(source, c, 0).wait_send()

    @pl.loop(1, n_chips)
    def _(d):
        rot_copy(r, peer(d), peer_send.at[d]).wait_send()

    @pl.loop(0, n_chips)
    def _(d):
        rot_copy(r, twin, twin_send.at[d]).wait_send()


def local(n_rows, n_bands, psi_panels, rotation, accumulated):
    psi, acc = psi_panels.T, accumulated.T
    kz, mrows = psi.shape
    kr, nb = rotation.shape
    chunks = mrows // CHUNK
    out = pl.pallas_call(
        functools.partial(kernel, n_rows, n_bands),
        out_shape=pltpu.VMEM((nb, mrows), jnp.float32),
        in_specs=[pl.BlockSpec(memory_space=pltpu.HBM)] * 3,
        out_specs=pl.BlockSpec(memory_space=pltpu.VMEM),
        scratch_shapes=[
            pltpu.VMEM((n_bands, kz, mrows), jnp.float32),
            pltpu.VMEM((n_rows, kr, nb), jnp.float32),
            pltpu.VMEM((nb, 3 * n_rows * kr), jnp.bfloat16),
            pltpu.SemaphoreType.DMA((n_bands, chunks)),
            pltpu.SemaphoreType.DMA((2, n_bands, chunks)),
            pltpu.SemaphoreType.DMA((n_rows,)),
            pltpu.SemaphoreType.DMA((n_rows // 2,)),
            pltpu.SemaphoreType.DMA((n_rows // 2,)),
            pltpu.SemaphoreType.DMA((3,)),
        ],
        compiler_params=pltpu.CompilerParams(
            collective_id=0, has_side_effects=True, vmem_limit_bytes=32 * 1024 * 1024),
        cost_estimate=pl.CostEstimate(
            flops=6 * nb * mrows * n_rows * kr, bytes_accessed=8 * nb * mrows, transcendentals=0),
        name="rotate",
    )(*(pltpu.with_memory_space_constraint(x, pltpu.HBM) for x in (psi, rotation, acc)))
    return out.T


def solution(mesh):
    sizes = mesh.shape["rows"], mesh.shape["bands"]
    specs = P("rows", "bands")
    return jax.shard_map(
        functools.partial(local, *sizes), mesh=mesh, in_specs=(specs,) * 3, out_specs=specs, check_vma=False)
```

```python
import functools

import jax
import jax.numpy as jnp
from jax import lax
from jax.experimental import pallas as pl
from jax.experimental.pallas import tpu as pltpu
from jax.sharding import PartitionSpec as P

MESH = pl.DeviceIdType.MESH
CHUNK = 256


def split(x):
    high = x.astype(jnp.bfloat16)
    low = (x - high.astype(jnp.float32)).astype(jnp.bfloat16)
    return high, low


def parts_of(n_rows):
    return 2 if n_rows == 8 else 1


def kernel(n_rows, n_bands, psi_ref, rot_ref, acc_ref, out_ref,
           psi_all, rot_all, rot_split,
           psi_recv, psi_send, rot_recv, peer_send, twin_send, local_sem):
    r = lax.axis_index("rows")
    z = lax.axis_index("bands")
    n_chips = n_rows // 2
    chip, core = r // 2, r % 2
    twin = 2 * chip + 1 - core
    kz, mrows = psi_ref.shape
    kr, nb = rot_ref.shape
    chunks = mrows // CHUNK
    square = n_chips == 4
    parts = parts_of(n_rows)
    x, y = chip % 2, chip // 2
    xn = 2 * (2 * y + 1 - x) + core
    yn = 2 * (2 * (1 - y) + x) + core
    dn = 2 * (2 * (1 - y) + 1 - x) + core

    def peer(d):
        return 2 * lax.rem(chip + d, n_chips) + core

    def columns(c):
        return pl.ds(pl.multiple_of(c * CHUNK, CHUNK), CHUNK)

    load_acc = pltpu.make_async_copy(acc_ref, out_ref, local_sem.at[0])
    load_psi = pltpu.make_async_copy(psi_ref, psi_all.at[z], local_sem.at[1])
    load_rot = pltpu.make_async_copy(rot_ref, rot_all.at[r], local_sem.at[2])

    barrier = pltpu.get_barrier_semaphore()

    def greet(rows, bands):
        pl.semaphore_signal(barrier, inc=1, device_id=(rows, bands), device_id_type=MESH)

    pl.when(z > 0)(lambda: greet(r, z - 1))
    pl.when(z < n_bands - 1)(lambda: greet(r, z + 1))
    greet(twin, z)

    @pl.loop(1, n_chips)
    def _(d):
        greet(peer(d), z)

    expected = n_chips + jnp.where(z > 0, 1, 0) + jnp.where(z < n_bands - 1, 1, 0)
    pl.semaphore_wait(barrier, expected)

    def psi_copy(source, c, way, own=False):
        here = psi_ref if own else psi_all.at[source]
        target = z + 2 * way - 1
        return pltpu.make_async_remote_copy(
            src_ref=here.at[:, columns(c)],
            dst_ref=psi_all.at[source, :, columns(c)],
            send_sem=psi_send.at[way, source, c],
            recv_sem=psi_recv.at[source, c],
            device_id=(r, target), device_id_type=MESH)

    def rot_copy(source, part, target, send_sem, own=False):
        here = rot_ref if own else rot_all.at[source]
        rows = pl.ds(part * (kr // parts), kr // parts)
        return pltpu.make_async_remote_copy(
            src_ref=here.at[rows],
            dst_ref=rot_all.at[source, rows],
            send_sem=send_sem, recv_sem=rot_recv.at[source, part],
            device_id=(target, z), device_id_type=MESH)

    def own_psi(c):
        pl.when(z > 0)(lambda: psi_copy(z, c, 0, own=True).start())
        pl.when(z < n_bands - 1)(lambda: psi_copy(z, c, 1, own=True).start())

    def own_psi_sent(c):
        pl.when(z > 0)(lambda: psi_copy(z, c, 0, own=True).wait_send())
        pl.when(z < n_bands - 1)(lambda: psi_copy(z, c, 1, own=True).wait_send())

    def pass_on(h, c):
        @pl.when((z - h >= 0) & (z + 1 < n_bands))
        def _():
            copy = psi_copy(z - h, c, 1)
            copy.wait_recv()
            copy.start()

        @pl.when((z + h < n_bands) & (z > 0))
        def _():
            copy = psi_copy(z + h, c, 0)
            copy.wait_recv()
            copy.start()

    def to_twin(source, part, d, wait=True):
        copy = rot_copy(source, part, twin, twin_send.at[d, part], own=not wait)
        if wait:
            copy.wait_recv()
        copy.start()

    for c in range(min(2, chunks)):
        own_psi(c)

    if square:
        sends = [(xn, 0, 1), (yn, 1, 2), (xn, 1, 1), (yn, 0, 2)]
        for target, part, d in sends:
            rot_copy(r, part, target, peer_send.at[d, part], own=True).start()
    else:
        @pl.loop(1, n_chips)
        def _(d):
            rot_copy(r, 0, peer(d), peer_send.at[d, 0], own=True).start()
    for part in range(parts):
        to_twin(r, part, 0, wait=False)
    load_psi.start()
    load_rot.start()
    load_acc.start()

    @pl.loop(2, chunks)
    def _(c):
        own_psi_sent(c - 2)
        own_psi(c)

    if n_bands > 3:
        @pl.loop(1, n_bands - 2)
        def _(h):
            pl.loop(0, chunks)(lambda c: pass_on(h, c))

    if square:
        for source, part, target, d in ((xn, 0, yn, 1), (yn, 1, xn, 2)):
            to_twin(source, part, d)
            rot_copy(source, part, target, peer_send.at[0, part]).start()
        to_twin(xn, 1, 1)
        to_twin(yn, 0, 2)
        for part in range(parts):
            to_twin(dn, part, 3)
    else:
        @pl.loop(1, n_chips)
        def _(d):
            to_twin(peer(n_chips - d), 0, d)

    if n_bands > 2:
        for c in range(min(2, chunks)):
            pass_on(n_bands - 2, c)

    @pl.loop(0, n_chips)
    def _(d):
        source = 2 * lax.rem(chip + d, n_chips) + 1 - core
        for part in range(parts):
            rot_copy(source, part, twin, twin_send.at[d, part]).wait_recv()

    load_rot.wait()
    for start in range(0, nb, 128):
        width = min(128, nb - start)
        block = rot_all[:, :, start:start + width].reshape(n_rows * kr, width).T
        high, low = split(block)
        rot_split[start:start + width, :] = jnp.concatenate([high, low, high], axis=1)

    load_psi.wait()
    load_acc.wait()

    @pl.loop(0, chunks)
    def _(c):
        if n_bands > 2:
            pl.when(c + 2 < chunks)(lambda: pass_on(n_bands - 2, c + 2))

        @pl.when(z == 0)
        def _():
            @pl.loop(1, n_bands)
            def _(source):
                psi_copy(source, c, 1).wait_recv()

        @pl.when(z == n_bands - 1)
        def _():
            @pl.loop(0, n_bands - 1)
            def _(source):
                psi_copy(source, c, 0).wait_recv()

        high, low = split(psi_all[:, :, columns(c)].reshape(n_bands * kz, CHUNK))
        operand = jnp.concatenate([high, high, low], axis=0)
        out_ref[:, columns(c)] += jnp.dot(
            rot_split[...], operand, preferred_element_type=jnp.float32)

    pl.loop(max(0, chunks - 2), chunks)(own_psi_sent)

    @pl.loop(0, chunks)
    def _(c):
        @pl.when(z < n_bands - 1)
        def _():
            @pl.loop(0, z)
            def _(source):
                psi_copy(source, c, 1).wait_send()

        @pl.when(z > 0)
        def _():
            @pl.loop(z + 1, n_bands)
            def _(source):
                psi_copy(source, c, 0).wait_send()

    if square:
        for target, part, d in sends + [(yn, 0, 0), (xn, 1, 0)]:
            rot_copy(r, part, target, peer_send.at[d, part]).wait_send()
    else:
        @pl.loop(1, n_chips)
        def _(d):
            rot_copy(r, 0, peer(d), peer_send.at[d, 0]).wait_send()

    @pl.loop(0, n_chips)
    def _(d):
        for part in range(parts):
            rot_copy(r, part, twin, twin_send.at[d, part]).wait_send()


def local(n_rows, n_bands, psi_panels, rotation, accumulated):
    psi, acc = psi_panels.T, accumulated.T
    kz, mrows = psi.shape
    kr, nb = rotation.shape
    chunks = mrows // CHUNK
    out = pl.pallas_call(
        functools.partial(kernel, n_rows, n_bands),
        out_shape=pltpu.VMEM((nb, mrows), jnp.float32),
        in_specs=[pl.BlockSpec(memory_space=pltpu.HBM)] * 3,
        out_specs=pl.BlockSpec(memory_space=pltpu.VMEM),
        scratch_shapes=[
            pltpu.VMEM((n_bands, kz, mrows), jnp.float32),
            pltpu.VMEM((n_rows, kr, nb), jnp.float32),
            pltpu.VMEM((nb, 3 * n_rows * kr), jnp.bfloat16),
            pltpu.SemaphoreType.DMA((n_bands, chunks)),
            pltpu.SemaphoreType.DMA((2, n_bands, chunks)),
            pltpu.SemaphoreType.DMA((n_rows, parts_of(n_rows))),
            pltpu.SemaphoreType.DMA((n_rows // 2, parts_of(n_rows))),
            pltpu.SemaphoreType.DMA((n_rows // 2, parts_of(n_rows))),
            pltpu.SemaphoreType.DMA((3,)),
        ],
        compiler_params=pltpu.CompilerParams(
            collective_id=0, has_side_effects=True, vmem_limit_bytes=32 * 1024 * 1024),
        cost_estimate=pl.CostEstimate(
            flops=6 * nb * mrows * n_rows * kr, bytes_accessed=8 * nb * mrows, transcendentals=0),
        name="rotate",
    )(*(pltpu.with_memory_space_constraint(x, pltpu.HBM) for x in (psi, rotation, acc)))
    return out.T


def solution(mesh):
    sizes = mesh.shape["rows"], mesh.shape["bands"]
    specs = P("rows", "bands")
    return jax.shard_map(
        functools.partial(local, *sizes), mesh=mesh, in_specs=(specs,) * 3, out_specs=specs, check_vma=False)
```

```python
import functools

import jax
import jax.numpy as jnp
from jax import lax
from jax.experimental import pallas as pl
from jax.experimental.pallas import tpu as pltpu
from jax.sharding import PartitionSpec as P

MESH = pl.DeviceIdType.MESH
CHUNK = 256


def split(x):
    high = x.astype(jnp.bfloat16)
    low = (x - high.astype(jnp.float32)).astype(jnp.bfloat16)
    return high, low


def rot_operand(block):
    high, low = split(block.T)
    return jnp.concatenate([high, low, high, low], axis=1)


def psi_operand(block):
    high, low = split(block)
    return jnp.concatenate([high, high, low, low], axis=0)


def parts_of(n_rows):
    return 2 if n_rows == 8 else 1


def kernel(n_rows, n_bands, psi_ref, rot_ref, acc_ref, out_ref, rot_late, psi_late,
           psi_all, rot_all, rot_early,
           psi_recv, psi_send, rot_recv, peer_send, twin_send, local_sem):
    r = lax.axis_index("rows")
    z = lax.axis_index("bands")
    n_chips = n_rows // 2
    chip, core = r // 2, r % 2
    twin = 2 * chip + 1 - core
    kz, mrows = psi_ref.shape
    kr, nb = rot_ref.shape
    chunks = mrows // CHUNK
    square = n_chips == 4
    parts = parts_of(n_rows)
    x, y = chip % 2, chip // 2
    xn = 2 * (2 * y + 1 - x) + core
    yn = 2 * (2 * (1 - y) + x) + core
    dn = 2 * (2 * (1 - y) + 1 - x) + core

    def peer(d):
        return 2 * lax.rem(chip + d, n_chips) + core

    def columns(c):
        return pl.ds(pl.multiple_of(c * CHUNK, CHUNK), CHUNK)

    load_acc = pltpu.make_async_copy(acc_ref, out_ref, local_sem.at[0])
    load_psi = pltpu.make_async_copy(psi_ref, psi_all.at[z], local_sem.at[1])
    load_rot = pltpu.make_async_copy(rot_ref, rot_all.at[r], local_sem.at[2])

    barrier = pltpu.get_barrier_semaphore()

    def greet(rows, bands):
        pl.semaphore_signal(barrier, inc=1, device_id=(rows, bands), device_id_type=MESH)

    pl.when(z > 0)(lambda: greet(r, z - 1))
    pl.when(z < n_bands - 1)(lambda: greet(r, z + 1))
    greet(twin, z)

    @pl.loop(1, n_chips)
    def _(d):
        greet(peer(d), z)

    expected = n_chips + jnp.where(z > 0, 1, 0) + jnp.where(z < n_bands - 1, 1, 0)
    pl.semaphore_wait(barrier, expected)

    def psi_copy(source, c, way, own=False):
        here = psi_ref if own else psi_all.at[source]
        target = z + 2 * way - 1
        return pltpu.make_async_remote_copy(
            src_ref=here.at[:, columns(c)],
            dst_ref=psi_all.at[source, :, columns(c)],
            send_sem=psi_send.at[way, source, c],
            recv_sem=psi_recv.at[source, c],
            device_id=(r, target), device_id_type=MESH)

    def rot_copy(source, part, target, send_sem, own=False):
        here = rot_ref if own else rot_all.at[source]
        rows = pl.ds(part * (kr // parts), kr // parts)
        return pltpu.make_async_remote_copy(
            src_ref=here.at[rows],
            dst_ref=rot_all.at[source, rows],
            send_sem=send_sem, recv_sem=rot_recv.at[source, part],
            device_id=(target, z), device_id_type=MESH)

    def own_psi(c):
        pl.when(z > 0)(lambda: psi_copy(z, c, 0, own=True).start())
        pl.when(z < n_bands - 1)(lambda: psi_copy(z, c, 1, own=True).start())

    def own_psi_sent(c):
        pl.when(z > 0)(lambda: psi_copy(z, c, 0, own=True).wait_send())
        pl.when(z < n_bands - 1)(lambda: psi_copy(z, c, 1, own=True).wait_send())

    def pass_on(h, c):
        @pl.when((z - h >= 0) & (z + 1 < n_bands))
        def _():
            copy = psi_copy(z - h, c, 1)
            copy.wait_recv()
            copy.start()

        @pl.when((z + h < n_bands) & (z > 0))
        def _():
            copy = psi_copy(z + h, c, 0)
            copy.wait_recv()
            copy.start()

    def to_twin(source, part, d, wait=True):
        copy = rot_copy(source, part, twin, twin_send.at[d, part], own=not wait)
        if wait:
            copy.wait_recv()
        copy.start()

    for c in range(min(2, chunks)):
        own_psi(c)

    if square:
        sends = [(xn, 0, 1), (yn, 1, 2), (xn, 1, 1), (yn, 0, 2)]
        for target, part, d in sends:
            rot_copy(r, part, target, peer_send.at[d, part], own=True).start()
    else:
        @pl.loop(1, n_chips)
        def _(d):
            rot_copy(r, 0, peer(d), peer_send.at[d, 0], own=True).start()
    for part in range(parts):
        to_twin(r, part, 0, wait=False)
    load_psi.start()
    load_rot.start()
    load_acc.start()

    @pl.loop(2, chunks)
    def _(c):
        own_psi_sent(c - 2)
        own_psi(c)

    if n_bands > 3:
        @pl.loop(1, n_bands - 2)
        def _(h):
            pl.loop(0, chunks)(lambda c: pass_on(h, c))

    if square:
        for source, part, target, d in ((xn, 0, yn, 1), (yn, 1, xn, 2)):
            to_twin(source, part, d)
            rot_copy(source, part, target, peer_send.at[0, part]).start()
        to_twin(xn, 1, 1)
        to_twin(yn, 0, 2)
        for part in range(parts):
            to_twin(dn, part, 3)
    else:
        @pl.loop(1, n_chips)
        def _(d):
            to_twin(peer(n_chips - d), 0, d)

    if n_bands > 2:
        for c in range(min(2, chunks)):
            pass_on(n_bands - 2, c)

    @pl.loop(0, n_chips)
    def _(d):
        source = 2 * lax.rem(chip + d, n_chips) + 1 - core
        for part in range(parts):
            rot_copy(source, part, twin, twin_send.at[d, part]).wait_recv()

    far_down = 2 * z >= n_bands
    late = jnp.where(far_down, 0, n_bands - 1)
    first = jnp.where(far_down, 1, 0)
    inward = jnp.where(far_down, 0, 1)
    per_band = n_rows // n_bands

    load_rot.wait()
    for start in range(0, nb, 128):
        width = min(128, nb - start)
        columns_here = slice(start, start + width)
        early = rot_all[pl.ds(first * per_band, n_rows - per_band), :, columns_here]
        rot_early[columns_here, :] = rot_operand(early.reshape(-1, width))
        last = rot_all[pl.ds(late * per_band, per_band), :, columns_here]
        rot_late[columns_here, :] = rot_operand(last.reshape(-1, width))

    load_psi.wait()
    load_acc.wait()

    @pl.loop(0, chunks)
    def _(c):
        if n_bands > 2:
            pl.when(c + 2 < chunks)(lambda: pass_on(n_bands - 2, c + 2))

        @pl.when((z == 0) | (z == n_bands - 1))
        def _():
            @pl.loop(1, n_bands - 1)
            def _(source):
                psi_copy(source, c, inward).wait_recv()

        early = psi_all[pl.ds(first, n_bands - 1), :, columns(c)]
        out_ref[:, columns(c)] += jnp.dot(
            rot_early[...], psi_operand(early.reshape(-1, CHUNK)), preferred_element_type=jnp.float32)

    @pl.loop(0, chunks)
    def _(c):
        @pl.when((z == 0) | (z == n_bands - 1))
        def _():
            psi_copy(late, c, inward).wait_recv()

        psi_late[:, columns(c)] = psi_operand(psi_all[late, :, columns(c)])

    pl.loop(max(0, chunks - 2), chunks)(own_psi_sent)

    @pl.loop(0, chunks)
    def _(c):
        @pl.when(z < n_bands - 1)
        def _():
            @pl.loop(0, z)
            def _(source):
                psi_copy(source, c, 1).wait_send()

        @pl.when(z > 0)
        def _():
            @pl.loop(z + 1, n_bands)
            def _(source):
                psi_copy(source, c, 0).wait_send()

    if square:
        for target, part, d in sends + [(yn, 0, 0), (xn, 1, 0)]:
            rot_copy(r, part, target, peer_send.at[d, part]).wait_send()
    else:
        @pl.loop(1, n_chips)
        def _(d):
            rot_copy(r, 0, peer(d), peer_send.at[d, 0]).wait_send()

    @pl.loop(0, n_chips)
    def _(d):
        for part in range(parts):
            rot_copy(r, part, twin, twin_send.at[d, part]).wait_send()


def finish(sum_ref, rot_ref, psi_ref, out_ref, held, sems):
    copies = []
    for c in range(held.shape[0]):
        columns = pl.ds(c * CHUNK, CHUNK)
        held[c] = sum_ref[:, columns] + jnp.dot(
            rot_ref[...], psi_ref[:, columns], preferred_element_type=jnp.float32)
        copies.append(pltpu.make_async_copy(held.at[c], out_ref.at[:, columns], sems.at[c]))
        copies[-1].start()
    for copy in copies:
        copy.wait()


def local(n_rows, n_bands, psi_panels, rotation, accumulated):
    psi, acc = psi_panels.T, accumulated.T
    kz, mrows = psi.shape
    kr, nb = rotation.shape
    chunks = mrows // CHUNK
    parts = parts_of(n_rows)
    vmem, hbm = pl.BlockSpec(memory_space=pltpu.VMEM), pl.BlockSpec(memory_space=pltpu.HBM)
    mib = 1024 * 1024
    partial = pl.pallas_call(
        functools.partial(kernel, n_rows, n_bands),
        out_shape=[
            pltpu.VMEM((nb, mrows), jnp.float32),
            pltpu.VMEM((nb, 4 * kz), jnp.bfloat16),
            pltpu.VMEM((4 * kz, mrows), jnp.bfloat16),
        ],
        in_specs=[hbm] * 3,
        out_specs=[vmem] * 3,
        scratch_shapes=[
            pltpu.VMEM((n_bands, kz, mrows), jnp.float32),
            pltpu.VMEM((n_rows, kr, nb), jnp.float32),
            pltpu.VMEM((nb, 4 * (n_bands - 1) * kz), jnp.bfloat16),
            pltpu.SemaphoreType.DMA((n_bands, chunks)),
            pltpu.SemaphoreType.DMA((2, n_bands, chunks)),
            pltpu.SemaphoreType.DMA((n_rows, parts)),
            pltpu.SemaphoreType.DMA((n_rows // 2, parts)),
            pltpu.SemaphoreType.DMA((n_rows // 2, parts)),
            pltpu.SemaphoreType.DMA((3,)),
        ],
        compiler_params=pltpu.CompilerParams(
            collective_id=0, has_side_effects=True, vmem_limit_bytes=24 * mib),
        cost_estimate=pl.CostEstimate(
            flops=6 * nb * mrows * n_rows * kr, bytes_accessed=4 * nb * mrows, transcendentals=0),
        name="rotate",
    )(*(pltpu.with_memory_space_constraint(x, pltpu.HBM) for x in (psi, rotation, acc)))
    out = pl.pallas_call(
        finish,
        out_shape=jax.ShapeDtypeStruct((nb, mrows), jnp.float32),
        in_specs=[vmem] * 3,
        out_specs=hbm,
        scratch_shapes=[
            pltpu.VMEM((chunks, nb, CHUNK), jnp.float32),
            pltpu.SemaphoreType.DMA((chunks,)),
        ],
        compiler_params=pltpu.CompilerParams(vmem_limit_bytes=24 * mib),
        cost_estimate=pl.CostEstimate(
            flops=8 * nb * mrows * kz, bytes_accessed=4 * nb * mrows, transcendentals=0),
        name="finish",
    )(*(pltpu.with_memory_space_constraint(x, pltpu.VMEM) for x in partial))
    return out.T


def solution(mesh):
    sizes = mesh.shape["rows"], mesh.shape["bands"]
    specs = P("rows", "bands")
    return jax.shard_map(
        functools.partial(local, *sizes), mesh=mesh, in_specs=(specs,) * 3, out_specs=specs, check_vma=False)
```

```python
import functools

import jax
import jax.numpy as jnp
from jax import lax
from jax.experimental import pallas as pl
from jax.experimental.pallas import tpu as pltpu
from jax.sharding import PartitionSpec as P

MESH = pl.DeviceIdType.MESH
CHUNK = 256
WIDE = 512


def split(x):
    high = x.astype(jnp.bfloat16)
    low = (x - high.astype(jnp.float32)).astype(jnp.bfloat16)
    return high, low


def block_rows(nb):
    fit = [rows for rows in range(16, 513, 16) if nb % rows == 0]
    return max(fit, default=nb)


def rot_operand(block):
    high, low = split(block.T)
    return jnp.concatenate([high, low, high, low], axis=1)


def psi_operand(block):
    high, low = split(block)
    return jnp.concatenate([high, high, low, low], axis=0)


def parts_of(n_rows):
    return 2 if n_rows == 8 else 1


def kernel(n_rows, n_bands, psi_ref, rot_ref, acc_ref, out_ref, rot_late, psi_late,
           psi_all, rot_all, rot_early, psi_early,
           psi_recv, psi_send, rot_recv, peer_send, twin_send, local_sem):
    r = lax.axis_index("rows")
    z = lax.axis_index("bands")
    n_chips = n_rows // 2
    chip, core = r // 2, r % 2
    twin = 2 * chip + 1 - core
    kz, mrows = psi_ref.shape
    kr, nb = rot_ref.shape
    chunks = mrows // CHUNK
    square = n_chips == 4
    parts = parts_of(n_rows)
    x, y = chip % 2, chip // 2
    xn = 2 * (2 * y + 1 - x) + core
    yn = 2 * (2 * (1 - y) + x) + core
    dn = 2 * (2 * (1 - y) + 1 - x) + core

    def peer(d):
        return 2 * lax.rem(chip + d, n_chips) + core

    def columns(c):
        return pl.ds(pl.multiple_of(c * CHUNK, CHUNK), CHUNK)

    load_acc = pltpu.make_async_copy(acc_ref, out_ref, local_sem.at[0])
    load_psi = pltpu.make_async_copy(psi_ref, psi_all.at[z], local_sem.at[1])
    load_rot = pltpu.make_async_copy(rot_ref, rot_all.at[r], local_sem.at[2])

    barrier = pltpu.get_barrier_semaphore()

    def greet(rows, bands):
        pl.semaphore_signal(barrier, inc=1, device_id=(rows, bands), device_id_type=MESH)

    pl.when(z > 0)(lambda: greet(r, z - 1))
    pl.when(z < n_bands - 1)(lambda: greet(r, z + 1))
    greet(twin, z)

    @pl.loop(1, n_chips)
    def _(d):
        greet(peer(d), z)

    expected = n_chips + jnp.where(z > 0, 1, 0) + jnp.where(z < n_bands - 1, 1, 0)
    pl.semaphore_wait(barrier, expected)

    def psi_copy(source, c, way, own=False):
        here = psi_ref if own else psi_all.at[source]
        target = z + 2 * way - 1
        return pltpu.make_async_remote_copy(
            src_ref=here.at[:, columns(c)],
            dst_ref=psi_all.at[source, :, columns(c)],
            send_sem=psi_send.at[way, source, c],
            recv_sem=psi_recv.at[source, c],
            device_id=(r, target), device_id_type=MESH)

    def rot_copy(source, part, target, send_sem, own=False):
        here = rot_ref if own else rot_all.at[source]
        rows = pl.ds(part * (kr // parts), kr // parts)
        return pltpu.make_async_remote_copy(
            src_ref=here.at[rows],
            dst_ref=rot_all.at[source, rows],
            send_sem=send_sem, recv_sem=rot_recv.at[source, part],
            device_id=(target, z), device_id_type=MESH)

    def own_psi(c):
        pl.when(z > 0)(lambda: psi_copy(z, c, 0, own=True).start())
        pl.when(z < n_bands - 1)(lambda: psi_copy(z, c, 1, own=True).start())

    def own_psi_sent(c):
        pl.when(z > 0)(lambda: psi_copy(z, c, 0, own=True).wait_send())
        pl.when(z < n_bands - 1)(lambda: psi_copy(z, c, 1, own=True).wait_send())

    def pass_on(h, c):
        @pl.when((z - h >= 0) & (z + 1 < n_bands))
        def _():
            copy = psi_copy(z - h, c, 1)
            copy.wait_recv()
            copy.start()

        @pl.when((z + h < n_bands) & (z > 0))
        def _():
            copy = psi_copy(z + h, c, 0)
            copy.wait_recv()
            copy.start()

    def to_twin(source, part, d, wait=True):
        copy = rot_copy(source, part, twin, twin_send.at[d, part], own=not wait)
        if wait:
            copy.wait_recv()
        copy.start()

    for c in range(min(2, chunks)):
        own_psi(c)

    if square:
        sends = [(xn, 0, 1), (yn, 1, 2), (xn, 1, 1), (yn, 0, 2)]
        for target, part, d in sends:
            rot_copy(r, part, target, peer_send.at[d, part], own=True).start()
    else:
        @pl.loop(1, n_chips)
        def _(d):
            rot_copy(r, 0, peer(d), peer_send.at[d, 0], own=True).start()
    for part in range(parts):
        to_twin(r, part, 0, wait=False)
    load_psi.start()
    load_rot.start()
    load_acc.start()

    @pl.loop(2, chunks)
    def _(c):
        own_psi_sent(c - 2)
        own_psi(c)

    if n_bands > 3:
        @pl.loop(1, n_bands - 2)
        def _(h):
            pl.loop(0, chunks)(lambda c: pass_on(h, c))

    if square:
        for source, part, target, d in ((xn, 0, yn, 1), (yn, 1, xn, 2)):
            to_twin(source, part, d)
            rot_copy(source, part, target, peer_send.at[0, part]).start()
        to_twin(xn, 1, 1)
        to_twin(yn, 0, 2)
        for part in range(parts):
            to_twin(dn, part, 3)
    else:
        @pl.loop(1, n_chips)
        def _(d):
            to_twin(peer(n_chips - d), 0, d)

    if n_bands > 2:
        for c in range(min(2, chunks)):
            pass_on(n_bands - 2, c)

    @pl.loop(0, n_chips)
    def _(d):
        source = 2 * lax.rem(chip + d, n_chips) + 1 - core
        for part in range(parts):
            rot_copy(source, part, twin, twin_send.at[d, part]).wait_recv()

    far_down = 2 * z >= n_bands
    late = jnp.where(far_down, 0, n_bands - 1)
    first = jnp.where(far_down, 1, 0)
    inward = jnp.where(far_down, 0, 1)
    per_band = n_rows // n_bands

    load_rot.wait()

    def make_operands(start, width):
        here = pl.ds(start, width)
        early = rot_all[pl.ds(first * per_band, n_rows - per_band), :, here]
        rot_early[here, :] = rot_operand(early.reshape(-1, width))
        last = rot_all[pl.ds(late * per_band, per_band), :, here]
        rot_late[here, :] = rot_operand(last.reshape(-1, width))

    @pl.loop(0, nb // 128)
    def _(i):
        make_operands(pl.multiple_of(i * 128, 128), 128)

    if nb % 128:
        make_operands(nb // 128 * 128, nb % 128)

    load_psi.wait()
    load_acc.wait()

    tall = block_rows(nb)
    blocks = nb // tall
    halves = mrows // WIDE
    per_half = WIDE // CHUNK

    @pl.loop(0, halves)
    def _(half):
        wide = pl.ds(pl.multiple_of(half * WIDE, WIDE), WIDE)

        @pl.when((z == 0) | (z == n_bands - 1))
        def _():
            @pl.loop(1, n_bands - 1)
            def _(source):
                for c in range(per_half):
                    psi_copy(source, half * per_half + c, inward).wait_recv()

        early = psi_all[pl.ds(first, n_bands - 1), :, wide]
        psi_early[...] = psi_operand(early.reshape(-1, WIDE))

        @pl.loop(0, blocks)
        def _(block):
            turn = half * blocks + block
            c = 2 + turn // 3
            if n_bands > 2:
                pl.when((turn % 3 == 0) & (c < chunks))(lambda: pass_on(n_bands - 2, c))
            rows = pl.ds(pl.multiple_of(block * tall, tall), tall)
            out_ref[rows, wide] += jnp.dot(
                rot_early[rows, :], psi_early[...], preferred_element_type=jnp.float32)

    if n_bands > 2:
        for c in range(2 + pl.cdiv(halves * blocks, 3), chunks):
            pass_on(n_bands - 2, c)

    @pl.loop(0, chunks)
    def _(c):
        @pl.when((z == 0) | (z == n_bands - 1))
        def _():
            psi_copy(late, c, inward).wait_recv()

        psi_late[:, columns(c)] = psi_operand(psi_all[late, :, columns(c)])

    pl.loop(max(0, chunks - 2), chunks)(own_psi_sent)

    @pl.loop(0, chunks)
    def _(c):
        @pl.when(z < n_bands - 1)
        def _():
            @pl.loop(0, z)
            def _(source):
                psi_copy(source, c, 1).wait_send()

        @pl.when(z > 0)
        def _():
            @pl.loop(z + 1, n_bands)
            def _(source):
                psi_copy(source, c, 0).wait_send()

    if square:
        for target, part, d in sends + [(yn, 0, 0), (xn, 1, 0)]:
            rot_copy(r, part, target, peer_send.at[d, part]).wait_send()
    else:
        @pl.loop(1, n_chips)
        def _(d):
            rot_copy(r, 0, peer(d), peer_send.at[d, 0]).wait_send()

    @pl.loop(0, n_chips)
    def _(d):
        for part in range(parts):
            rot_copy(r, part, twin, twin_send.at[d, part]).wait_send()


def finish(sum_ref, rot_ref, psi_ref, out_ref, held, sems):
    blocks, tall, _ = held.shape

    def write(block):
        rows = pl.ds(pl.multiple_of(block * tall, tall), tall)
        return pltpu.make_async_copy(held.at[block], out_ref.at[rows], sems.at[block])

    @pl.loop(0, blocks)
    def _(block):
        rows = pl.ds(pl.multiple_of(block * tall, tall), tall)
        held[block] = sum_ref[rows, :] + jnp.dot(
            rot_ref[rows, :], psi_ref[...], preferred_element_type=jnp.float32)
        write(block).start()

    pl.loop(0, blocks)(lambda block: write(block).wait())


def local(n_rows, n_bands, psi_panels, rotation, accumulated):
    psi, acc = psi_panels.T, accumulated.T
    kz, mrows = psi.shape
    kr, nb = rotation.shape
    chunks = mrows // CHUNK
    parts = parts_of(n_rows)
    tall = block_rows(nb)
    vmem, hbm = pl.BlockSpec(memory_space=pltpu.VMEM), pl.BlockSpec(memory_space=pltpu.HBM)
    mib = 1024 * 1024
    partial = pl.pallas_call(
        functools.partial(kernel, n_rows, n_bands),
        out_shape=[
            pltpu.VMEM((nb, mrows), jnp.float32),
            pltpu.VMEM((nb, 4 * kz), jnp.bfloat16),
            pltpu.VMEM((4 * kz, mrows), jnp.bfloat16),
        ],
        in_specs=[hbm] * 3,
        out_specs=[vmem] * 3,
        scratch_shapes=[
            pltpu.VMEM((n_bands, kz, mrows), jnp.float32),
            pltpu.VMEM((n_rows, kr, nb), jnp.float32),
            pltpu.VMEM((nb, 4 * (n_bands - 1) * kz), jnp.bfloat16),
            pltpu.VMEM((4 * (n_bands - 1) * kz, WIDE), jnp.bfloat16),
            pltpu.SemaphoreType.DMA((n_bands, chunks)),
            pltpu.SemaphoreType.DMA((2, n_bands, chunks)),
            pltpu.SemaphoreType.DMA((n_rows, parts)),
            pltpu.SemaphoreType.DMA((n_rows // 2, parts)),
            pltpu.SemaphoreType.DMA((n_rows // 2, parts)),
            pltpu.SemaphoreType.DMA((3,)),
        ],
        compiler_params=pltpu.CompilerParams(
            collective_id=0, has_side_effects=True, vmem_limit_bytes=24 * mib),
        cost_estimate=pl.CostEstimate(
            flops=6 * nb * mrows * n_rows * kr, bytes_accessed=4 * nb * mrows, transcendentals=0),
        name="rotate",
    )(*(pltpu.with_memory_space_constraint(x, pltpu.HBM) for x in (psi, rotation, acc)))
    out = pl.pallas_call(
        finish,
        out_shape=jax.ShapeDtypeStruct((nb, mrows), jnp.float32),
        in_specs=[vmem] * 3,
        out_specs=hbm,
        scratch_shapes=[
            pltpu.VMEM((nb // tall, tall, mrows), jnp.float32),
            pltpu.SemaphoreType.DMA((nb // tall,)),
        ],
        compiler_params=pltpu.CompilerParams(vmem_limit_bytes=24 * mib),
        cost_estimate=pl.CostEstimate(
            flops=8 * nb * mrows * kz, bytes_accessed=4 * nb * mrows, transcendentals=0),
        name="finish",
    )(*(pltpu.with_memory_space_constraint(x, pltpu.VMEM) for x in partial))
    return out.T


def solution(mesh):
    sizes = mesh.shape["rows"], mesh.shape["bands"]
    specs = P("rows", "bands")
    return jax.shard_map(
        functools.partial(local, *sizes), mesh=mesh, in_specs=(specs,) * 3, out_specs=specs, check_vma=False)
```

```python
import functools

import jax
import jax.numpy as jnp
from jax import lax
from jax.experimental import pallas as pl
from jax.experimental.pallas import tpu as pltpu
from jax.sharding import PartitionSpec as P

MESH = pl.DeviceIdType.MESH
CHUNK = 256


def split(x):
    high = x.astype(jnp.bfloat16)
    low = (x - high.astype(jnp.float32)).astype(jnp.bfloat16)
    return high, low


def block_rows(nb):
    fit = [rows for rows in range(16, 513, 16) if nb % rows == 0]
    return max(fit, default=nb)


def rot_operand(block):
    high = block.astype(jnp.bfloat16).astype(jnp.float32)
    both = jnp.concatenate([high, block - high], axis=0).T.astype(jnp.bfloat16)
    return jnp.concatenate([both, both], axis=1)


def psi_operand(block):
    high, low = split(block)
    return jnp.concatenate([high, high, low, low], axis=0)


def parts_of(n_rows):
    return 2 if n_rows == 8 else 1


def kernel(n_rows, n_bands, psi_ref, rot_ref, acc_ref, out_ref, rot_op, psi_late,
           psi_all, rot_all, psi_early,
           psi_recv, psi_send, rot_recv, peer_send, twin_send, local_sem):
    r = lax.axis_index("rows")
    z = lax.axis_index("bands")
    n_chips = n_rows // 2
    chip, core = r // 2, r % 2
    twin = 2 * chip + 1 - core
    kz, mrows = psi_ref.shape
    kr, nb = rot_ref.shape
    chunks = mrows // CHUNK
    square = n_chips == 4
    parts = parts_of(n_rows)
    x, y = chip % 2, chip // 2
    xn = 2 * (2 * y + 1 - x) + core
    yn = 2 * (2 * (1 - y) + x) + core
    dn = 2 * (2 * (1 - y) + 1 - x) + core

    def peer(d):
        return 2 * lax.rem(chip + d, n_chips) + core

    def columns(c):
        return pl.ds(pl.multiple_of(c * CHUNK, CHUNK), CHUNK)

    load_acc = pltpu.make_async_copy(acc_ref, out_ref, local_sem.at[0])
    load_psi = pltpu.make_async_copy(psi_ref, psi_all.at[z], local_sem.at[1])
    load_rot = pltpu.make_async_copy(rot_ref, rot_all.at[r], local_sem.at[2])

    barrier = pltpu.get_barrier_semaphore()

    def greet(rows, bands):
        pl.semaphore_signal(barrier, inc=1, device_id=(rows, bands), device_id_type=MESH)

    pl.when(z > 0)(lambda: greet(r, z - 1))
    pl.when(z < n_bands - 1)(lambda: greet(r, z + 1))
    greet(twin, z)

    @pl.loop(1, n_chips)
    def _(d):
        greet(peer(d), z)

    expected = n_chips + jnp.where(z > 0, 1, 0) + jnp.where(z < n_bands - 1, 1, 0)
    pl.semaphore_wait(barrier, expected)

    def psi_copy(source, c, way, own=False):
        here = psi_ref if own else psi_all.at[source]
        target = z + 2 * way - 1
        return pltpu.make_async_remote_copy(
            src_ref=here.at[:, columns(c)],
            dst_ref=psi_all.at[source, :, columns(c)],
            send_sem=psi_send.at[way, source, c],
            recv_sem=psi_recv.at[source, c],
            device_id=(r, target), device_id_type=MESH)

    def rot_copy(source, part, target, send_sem, own=False):
        here = rot_ref if own else rot_all.at[source]
        rows = pl.ds(part * (kr // parts), kr // parts)
        return pltpu.make_async_remote_copy(
            src_ref=here.at[rows],
            dst_ref=rot_all.at[source, rows],
            send_sem=send_sem, recv_sem=rot_recv.at[source, part],
            device_id=(target, z), device_id_type=MESH)

    def own_psi(c):
        pl.when(z > 0)(lambda: psi_copy(z, c, 0, own=True).start())
        pl.when(z < n_bands - 1)(lambda: psi_copy(z, c, 1, own=True).start())

    def own_psi_sent(c):
        pl.when(z > 0)(lambda: psi_copy(z, c, 0, own=True).wait_send())
        pl.when(z < n_bands - 1)(lambda: psi_copy(z, c, 1, own=True).wait_send())

    def pass_on(h, c):
        @pl.when((z - h >= 0) & (z + 1 < n_bands))
        def _():
            copy = psi_copy(z - h, c, 1)
            copy.wait_recv()
            copy.start()

        @pl.when((z + h < n_bands) & (z > 0))
        def _():
            copy = psi_copy(z + h, c, 0)
            copy.wait_recv()
            copy.start()

    def to_twin(source, part, d, wait=True):
        copy = rot_copy(source, part, twin, twin_send.at[d, part], own=not wait)
        if wait:
            copy.wait_recv()
        copy.start()

    for c in range(min(2, chunks)):
        own_psi(c)

    if square:
        sends = [(xn, 0, 1), (yn, 1, 2), (xn, 1, 1), (yn, 0, 2)]
        for target, part, d in sends:
            rot_copy(r, part, target, peer_send.at[d, part], own=True).start()
    else:
        @pl.loop(1, n_chips)
        def _(d):
            rot_copy(r, 0, peer(d), peer_send.at[d, 0], own=True).start()
    for part in range(parts):
        to_twin(r, part, 0, wait=False)
    load_psi.start()
    load_rot.start()
    load_acc.start()

    @pl.loop(2, chunks)
    def _(c):
        own_psi_sent(c - 2)
        own_psi(c)

    def make_operand(s):
        def columns_from(start, width):
            here = pl.ds(start, width)
            block = rot_all[pl.ds(2 * s, 2), :, here].reshape(kz, width)
            rot_op[s, here, :] = rot_operand(block)

        full = nb // 128
        group = 5 if full % 5 == 0 else 1

        @pl.loop(0, full // group)
        def _(i):
            for j in range(group):
                columns_from(pl.multiple_of((i * group + j) * 128, 128), 128)

        if nb % 128:
            columns_from(full * 128, nb % 128)

    def from_twin(s):
        for part in range(parts):
            rot_copy(2 * s + 1 - core, part, twin, twin_send.at[0, part]).wait_recv()

    load_rot.wait()
    from_twin(chip)
    make_operand(chip)

    last_hop = n_bands - 2
    if n_bands > 3:
        for c in range(min(2, chunks)):
            pass_on(1, c)
    if square:
        for source, part, target, d in ((xn, 0, yn, 1), (yn, 1, xn, 2)):
            to_twin(source, part, d)
            rot_copy(source, part, target, peer_send.at[0, part]).start()
    if n_bands > 3:
        for c in range(2, chunks):
            pass_on(1, c)

        @pl.loop(2, last_hop)
        def _(h):
            pl.loop(0, chunks)(lambda c: pass_on(h, c))

    if square:
        to_twin(xn, 1, 1)
        to_twin(yn, 0, 2)
        for s in (xn // 2, yn // 2):
            from_twin(s)
            make_operand(s)
        if n_bands > 2:
            for c in range(min(2, chunks)):
                pass_on(last_hop, c)
        for part in range(parts):
            to_twin(dn, part, 3)
        from_twin(dn // 2)
        make_operand(dn // 2)
    else:
        @pl.loop(1, n_chips)
        def _(d):
            to_twin(peer(n_chips - d), 0, d)

        if n_bands > 2:
            for c in range(min(2, chunks)):
                pass_on(last_hop, c)

        @pl.loop(1, n_chips)
        def _(d):
            s = lax.rem(chip + d, n_chips)
            from_twin(s)
            make_operand(s)

    far_down = 2 * z >= n_bands
    late = jnp.where(far_down, 0, n_bands - 1)
    first = jnp.where(far_down, 1, 0)
    inward = jnp.where(far_down, 0, 1)
    at_end = (z == 0) | (z == n_bands - 1)

    load_psi.wait()

    @pl.when(at_end)
    def _():
        @pl.loop(1, n_bands - 1)
        def _(source):
            pl.loop(0, chunks)(lambda c: psi_copy(source, c, inward).wait_recv())

    @pl.loop(0, n_bands - 1)
    def _(j):
        psi_early[j] = psi_operand(psi_all[first + j])

    load_acc.wait()
    tall = block_rows(nb)
    blocks = nb // tall

    @pl.loop(0, blocks)
    def _(block):
        if n_bands > 2:
            pl.when(block + 2 < chunks)(lambda: pass_on(last_hop, block + 2))
        rows = pl.ds(pl.multiple_of(block * tall, tall), tall)
        left = jnp.concatenate([rot_op[first + j, rows, :] for j in range(n_bands - 1)], axis=1)
        out_ref[rows, :] += jnp.dot(
            left, psi_early[...].reshape(-1, mrows), preferred_element_type=jnp.float32)

    if n_bands > 2:
        for c in range(2 + blocks, chunks):
            pass_on(last_hop, c)

    @pl.loop(0, chunks)
    def _(c):
        pl.when(at_end)(lambda: psi_copy(late, c, inward).wait_recv())
        psi_late[:, columns(c)] = psi_operand(psi_all[late, :, columns(c)])

    pl.loop(max(0, chunks - 2), chunks)(own_psi_sent)

    @pl.loop(0, chunks)
    def _(c):
        @pl.when(z < n_bands - 1)
        def _():
            @pl.loop(0, z)
            def _(source):
                psi_copy(source, c, 1).wait_send()

        @pl.when(z > 0)
        def _():
            @pl.loop(z + 1, n_bands)
            def _(source):
                psi_copy(source, c, 0).wait_send()

    if square:
        for target, part, d in sends + [(yn, 0, 0), (xn, 1, 0)]:
            rot_copy(r, part, target, peer_send.at[d, part]).wait_send()
    else:
        @pl.loop(1, n_chips)
        def _(d):
            rot_copy(r, 0, peer(d), peer_send.at[d, 0]).wait_send()

    @pl.loop(0, n_chips)
    def _(d):
        for part in range(parts):
            rot_copy(r, part, twin, twin_send.at[d, part]).wait_send()


def finish(n_bands, sum_ref, rot_ref, psi_ref, out_ref, held, sems):
    blocks, tall, _ = held.shape
    late = jnp.where(2 * lax.axis_index("bands") >= n_bands, 0, n_bands - 1)

    def write(block):
        rows = pl.ds(pl.multiple_of(block * tall, tall), tall)
        return pltpu.make_async_copy(held.at[block], out_ref.at[rows], sems.at[block])

    @pl.loop(0, blocks)
    def _(block):
        rows = pl.ds(pl.multiple_of(block * tall, tall), tall)
        held[block] = sum_ref[rows, :] + jnp.dot(
            rot_ref[late, rows, :], psi_ref[...], preferred_element_type=jnp.float32)
        write(block).start()

    pl.loop(0, blocks)(lambda block: write(block).wait())


def local(n_rows, n_bands, psi_panels, rotation, accumulated):
    psi, acc = psi_panels.T, accumulated.T
    kz, mrows = psi.shape
    kr, nb = rotation.shape
    chunks = mrows // CHUNK
    parts = parts_of(n_rows)
    tall = block_rows(nb)
    vmem, hbm = pl.BlockSpec(memory_space=pltpu.VMEM), pl.BlockSpec(memory_space=pltpu.HBM)
    mib = 1024 * 1024
    partial = pl.pallas_call(
        functools.partial(kernel, n_rows, n_bands),
        out_shape=[
            pltpu.VMEM((nb, mrows), jnp.float32),
            pltpu.VMEM((n_bands, nb, 4 * kz), jnp.bfloat16),
            pltpu.VMEM((4 * kz, mrows), jnp.bfloat16),
        ],
        in_specs=[hbm] * 3,
        out_specs=[vmem] * 3,
        scratch_shapes=[
            pltpu.VMEM((n_bands, kz, mrows), jnp.float32),
            pltpu.VMEM((n_rows, kr, nb), jnp.float32),
            pltpu.VMEM((n_bands - 1, 4 * kz, mrows), jnp.bfloat16),
            pltpu.SemaphoreType.DMA((n_bands, chunks)),
            pltpu.SemaphoreType.DMA((2, n_bands, chunks)),
            pltpu.SemaphoreType.DMA((n_rows, parts)),
            pltpu.SemaphoreType.DMA((n_rows // 2, parts)),
            pltpu.SemaphoreType.DMA((n_rows // 2, parts)),
            pltpu.SemaphoreType.DMA((3,)),
        ],
        compiler_params=pltpu.CompilerParams(
            collective_id=0, has_side_effects=True, vmem_limit_bytes=24 * mib),
        cost_estimate=pl.CostEstimate(
            flops=6 * nb * mrows * n_rows * kr, bytes_accessed=4 * nb * mrows, transcendentals=0),
        name="rotate",
    )(*(pltpu.with_memory_space_constraint(x, pltpu.HBM) for x in (psi, rotation, acc)))
    out = pl.pallas_call(
        functools.partial(finish, n_bands),
        out_shape=jax.ShapeDtypeStruct((nb, mrows), jnp.float32),
        in_specs=[vmem] * 3,
        out_specs=hbm,
        scratch_shapes=[
            pltpu.VMEM((nb // tall, tall, mrows), jnp.float32),
            pltpu.SemaphoreType.DMA((nb // tall,)),
        ],
        compiler_params=pltpu.CompilerParams(vmem_limit_bytes=24 * mib),
        cost_estimate=pl.CostEstimate(
            flops=8 * nb * mrows * kz, bytes_accessed=4 * nb * mrows, transcendentals=0),
        name="finish",
    )(*(pltpu.with_memory_space_constraint(x, pltpu.VMEM) for x in partial))
    return out.T


def solution(mesh):
    sizes = mesh.shape["rows"], mesh.shape["bands"]
    specs = P("rows", "bands")
    return jax.shard_map(
        functools.partial(local, *sizes), mesh=mesh, in_specs=(specs,) * 3, out_specs=specs, check_vma=False)
```

```python
import functools

import jax
import jax.numpy as jnp
from jax import lax
from jax.experimental import pallas as pl
from jax.experimental.pallas import tpu as pltpu
from jax.sharding import PartitionSpec as P

MESH = pl.DeviceIdType.MESH


def split(x):
    high = x.astype(jnp.bfloat16)
    low = (x - high.astype(jnp.float32)).astype(jnp.bfloat16)
    return high, low


def chunks_of(kz):
    return max(n for n in (1, 2, 4) if kz % (8 * n) == 0)


def block_rows(nb):
    fit = [rows for rows in range(16, 513, 16) if nb % rows == 0]
    return max(fit, default=nb)


def rot_operand(block):
    high = block.astype(jnp.bfloat16).astype(jnp.float32)
    both = jnp.concatenate([high, block - high], axis=0).T.astype(jnp.bfloat16)
    return jnp.concatenate([both, both], axis=1)


def psi_operand(block):
    high, low = split(block)
    return jnp.concatenate([high, high, low, low], axis=0)


def parts_of(n_rows):
    return 2 if n_rows == 8 else 1


def kernel(n_rows, n_bands, psi_ref, rot_ref, acc_ref, out_ref, rot_op, psi_late,
           psi_all, rot_all, psi_early,
           psi_recv, psi_send, rot_recv, peer_send, twin_send, local_sem):
    r = lax.axis_index("rows")
    z = lax.axis_index("bands")
    n_chips = n_rows // 2
    chip, core = r // 2, r % 2
    twin = 2 * chip + 1 - core
    kz, mrows = psi_ref.shape
    kr, nb = rot_ref.shape
    chunks = chunks_of(kz)
    square = n_chips == 4
    parts = parts_of(n_rows)
    x, y = chip % 2, chip // 2
    xn = 2 * (2 * y + 1 - x) + core
    yn = 2 * (2 * (1 - y) + x) + core
    dn = 2 * (2 * (1 - y) + 1 - x) + core

    def peer(d):
        return 2 * lax.rem(chip + d, n_chips) + core

    def panel_rows(c):
        return pl.ds(pl.multiple_of(c * (kz // chunks), kz // chunks), kz // chunks)

    load_acc = pltpu.make_async_copy(acc_ref, out_ref, local_sem.at[0])
    load_psi = pltpu.make_async_copy(psi_ref, psi_all.at[z], local_sem.at[1])
    load_rot = pltpu.make_async_copy(rot_ref, rot_all.at[r], local_sem.at[2])

    barrier = pltpu.get_barrier_semaphore()

    def greet(rows, bands):
        pl.semaphore_signal(barrier, inc=1, device_id=(rows, bands), device_id_type=MESH)

    pl.when(z > 0)(lambda: greet(r, z - 1))
    pl.when(z < n_bands - 1)(lambda: greet(r, z + 1))
    greet(twin, z)

    @pl.loop(1, n_chips)
    def _(d):
        greet(peer(d), z)

    expected = n_chips + jnp.where(z > 0, 1, 0) + jnp.where(z < n_bands - 1, 1, 0)
    pl.semaphore_wait(barrier, expected)

    def psi_copy(source, c, way, own=False):
        here = psi_ref if own else psi_all.at[source]
        target = z + 2 * way - 1
        return pltpu.make_async_remote_copy(
            src_ref=here.at[panel_rows(c)],
            dst_ref=psi_all.at[source, panel_rows(c)],
            send_sem=psi_send.at[way, source, c],
            recv_sem=psi_recv.at[source, c],
            device_id=(r, target), device_id_type=MESH)

    def rot_copy(source, part, target, send_sem, own=False):
        here = rot_ref if own else rot_all.at[source]
        rows = pl.ds(part * (kr // parts), kr // parts)
        return pltpu.make_async_remote_copy(
            src_ref=here.at[rows],
            dst_ref=rot_all.at[source, rows],
            send_sem=send_sem, recv_sem=rot_recv.at[source, part],
            device_id=(target, z), device_id_type=MESH)

    def own_psi(c):
        pl.when(z > 0)(lambda: psi_copy(z, c, 0, own=True).start())
        pl.when(z < n_bands - 1)(lambda: psi_copy(z, c, 1, own=True).start())

    def own_psi_sent(c):
        pl.when(z > 0)(lambda: psi_copy(z, c, 0, own=True).wait_send())
        pl.when(z < n_bands - 1)(lambda: psi_copy(z, c, 1, own=True).wait_send())

    def pass_on(h, c):
        @pl.when((z - h >= 0) & (z + 1 < n_bands))
        def _():
            copy = psi_copy(z - h, c, 1)
            copy.wait_recv()
            copy.start()

        @pl.when((z + h < n_bands) & (z > 0))
        def _():
            copy = psi_copy(z + h, c, 0)
            copy.wait_recv()
            copy.start()

    def to_twin(source, part, d, wait=True):
        copy = rot_copy(source, part, twin, twin_send.at[d, part], own=not wait)
        if wait:
            copy.wait_recv()
        copy.start()

    for c in range(min(2, chunks)):
        own_psi(c)

    if square:
        sends = [(xn, 0, 1), (yn, 1, 2), (xn, 1, 1), (yn, 0, 2)]
        for target, part, d in sends:
            rot_copy(r, part, target, peer_send.at[d, part], own=True).start()
    else:
        @pl.loop(1, n_chips)
        def _(d):
            rot_copy(r, 0, peer(d), peer_send.at[d, 0], own=True).start()
    for part in range(parts):
        to_twin(r, part, 0, wait=False)
    load_psi.start()
    load_rot.start()
    load_acc.start()

    @pl.loop(2, chunks)
    def _(c):
        own_psi_sent(c - 2)
        own_psi(c)

    def make_operand(s):
        def columns_from(start, width):
            here = pl.ds(start, width)
            block = rot_all[pl.ds(2 * s, 2), :, here].reshape(kz, width)
            rot_op[s, here, :] = rot_operand(block)

        full = nb // 128
        group = 5 if full % 5 == 0 else 1

        @pl.loop(0, full // group)
        def _(i):
            for j in range(group):
                columns_from(pl.multiple_of((i * group + j) * 128, 128), 128)

        if nb % 128:
            columns_from(full * 128, nb % 128)

    def from_twin(s):
        for part in range(parts):
            rot_copy(2 * s + 1 - core, part, twin, twin_send.at[0, part]).wait_recv()

    load_rot.wait()
    from_twin(chip)
    make_operand(chip)

    last_hop = n_bands - 2
    if n_bands > 3:
        for c in range(min(2, chunks)):
            pass_on(1, c)
    if square:
        for source, part, target, d in ((xn, 0, yn, 1), (yn, 1, xn, 2)):
            to_twin(source, part, d)
            rot_copy(source, part, target, peer_send.at[0, part]).start()
    if n_bands > 3:
        for c in range(2, chunks):
            pass_on(1, c)

        @pl.loop(2, last_hop)
        def _(h):
            pl.loop(0, chunks)(lambda c: pass_on(h, c))

    far_down = 2 * z >= n_bands
    late = jnp.where(far_down, 0, n_bands - 1)
    first = jnp.where(far_down, 1, 0)
    inward = jnp.where(far_down, 0, 1)
    at_end = (z == 0) | (z == n_bands - 1)
    tall = block_rows(nb)
    blocks = nb // tall

    def arrived(source):
        pl.loop(0, chunks)(lambda c: psi_copy(source, c, inward).wait_recv())

    def add_products(sources, meanwhile):
        n = len(sources)
        for j, source in enumerate(sources):
            psi_early[j] = psi_operand(psi_all[source])

        @pl.loop(0, blocks)
        def _(block):
            meanwhile(block)
            rows = pl.ds(pl.multiple_of(block * tall, tall), tall)
            left = jnp.concatenate([rot_op[source, rows, :] for source in sources], axis=1)
            out_ref[rows, :] += jnp.dot(
                left, psi_early[0:n].reshape(-1, mrows), preferred_element_type=jnp.float32)

    def last_hop_at(block):
        if n_bands > 2:
            pl.when(block + 2 < chunks)(lambda: pass_on(last_hop, block + 2))

    if square and n_bands > 3:
        to_twin(xn, 1, 1)
        to_twin(yn, 0, 2)
        for s in (xn // 2, yn // 2):
            from_twin(s)
            make_operand(s)
        load_psi.wait()
        load_acc.wait()
        inner = jnp.where(far_down, z - 1, z + 1)
        soon = jnp.where(z == dn // 2, inner, z)
        pl.when(at_end)(lambda: arrived(inner))

        def first_two(block):
            pl.when(block == 0)(lambda: pass_on(last_hop, 0))
            pl.when(block == 2)(lambda: pass_on(last_hop, 1))

        add_products([soon], first_two)
        for c in (0, 1):
            if 2 * c >= blocks:
                pass_on(last_hop, c)
        for part in range(parts):
            to_twin(dn, part, 3)

        @pl.when(at_end)
        def _():
            @pl.loop(0, n_bands - 3)
            def _(j):
                arrived(j + 2 - first)

        from_twin(dn // 2)
        make_operand(dn // 2)
        rest = [first + j + jnp.where(first + j >= soon, 1, 0) for j in range(n_bands - 2)]
    else:
        @pl.loop(1, n_chips)
        def _(d):
            source = peer(n_chips - d)
            for part in range(parts):
                to_twin(source, part, d)

        if n_bands > 2:
            for c in range(min(2, chunks)):
                pass_on(last_hop, c)

        @pl.loop(1, n_chips)
        def _(d):
            s = lax.rem(chip + d, n_chips)
            from_twin(s)
            make_operand(s)

        load_psi.wait()
        load_acc.wait()

        @pl.when(at_end)
        def _():
            pl.loop(1, n_bands - 1)(arrived)

        rest = [first + j for j in range(n_bands - 1)]

    add_products(rest, last_hop_at)
    if n_bands > 2:
        for c in range(2 + blocks, chunks):
            pass_on(last_hop, c)

    pl.when(at_end)(lambda: arrived(late))
    psi_late[...] = psi_operand(psi_all[late])

    pl.loop(max(0, chunks - 2), chunks)(own_psi_sent)

    @pl.loop(0, chunks)
    def _(c):
        @pl.when(z < n_bands - 1)
        def _():
            @pl.loop(0, z)
            def _(source):
                psi_copy(source, c, 1).wait_send()

        @pl.when(z > 0)
        def _():
            @pl.loop(z + 1, n_bands)
            def _(source):
                psi_copy(source, c, 0).wait_send()

    if square:
        for target, part, d in sends + [(yn, 0, 0), (xn, 1, 0)]:
            rot_copy(r, part, target, peer_send.at[d, part]).wait_send()
    else:
        @pl.loop(1, n_chips)
        def _(d):
            rot_copy(r, 0, peer(d), peer_send.at[d, 0]).wait_send()

    @pl.loop(0, n_chips)
    def _(d):
        for part in range(parts):
            rot_copy(r, part, twin, twin_send.at[d, part]).wait_send()


def finish(n_bands, sum_ref, rot_ref, psi_ref, out_ref, held, sems):
    blocks, tall, _ = held.shape
    late = jnp.where(2 * lax.axis_index("bands") >= n_bands, 0, n_bands - 1)

    def write(block):
        rows = pl.ds(pl.multiple_of(block * tall, tall), tall)
        return pltpu.make_async_copy(held.at[block], out_ref.at[rows], sems.at[block])

    @pl.loop(0, blocks)
    def _(block):
        rows = pl.ds(pl.multiple_of(block * tall, tall), tall)
        held[block] = sum_ref[rows, :] + jnp.dot(
            rot_ref[late, rows, :], psi_ref[...], preferred_element_type=jnp.float32)
        write(block).start()

    pl.loop(0, blocks)(lambda block: write(block).wait())


def local(n_rows, n_bands, psi_panels, rotation, accumulated):
    psi, acc = psi_panels.T, accumulated.T
    kz, mrows = psi.shape
    kr, nb = rotation.shape
    chunks = chunks_of(kz)
    parts = parts_of(n_rows)
    tall = block_rows(nb)
    vmem, hbm = pl.BlockSpec(memory_space=pltpu.VMEM), pl.BlockSpec(memory_space=pltpu.HBM)
    mib = 1024 * 1024
    partial = pl.pallas_call(
        functools.partial(kernel, n_rows, n_bands),
        out_shape=[
            pltpu.VMEM((nb, mrows), jnp.float32),
            pltpu.VMEM((n_bands, nb, 4 * kz), jnp.bfloat16),
            pltpu.VMEM((4 * kz, mrows), jnp.bfloat16),
        ],
        in_specs=[hbm] * 3,
        out_specs=[vmem] * 3,
        scratch_shapes=[
            pltpu.VMEM((n_bands, kz, mrows), jnp.float32),
            pltpu.VMEM((n_rows, kr, nb), jnp.float32),
            pltpu.VMEM((n_bands - 1, 4 * kz, mrows), jnp.bfloat16),
            pltpu.SemaphoreType.DMA((n_bands, chunks)),
            pltpu.SemaphoreType.DMA((2, n_bands, chunks)),
            pltpu.SemaphoreType.DMA((n_rows, parts)),
            pltpu.SemaphoreType.DMA((n_rows // 2, parts)),
            pltpu.SemaphoreType.DMA((n_rows // 2, parts)),
            pltpu.SemaphoreType.DMA((3,)),
        ],
        compiler_params=pltpu.CompilerParams(
            collective_id=0, has_side_effects=True, vmem_limit_bytes=24 * mib),
        cost_estimate=pl.CostEstimate(
            flops=6 * nb * mrows * n_rows * kr, bytes_accessed=4 * nb * mrows, transcendentals=0),
        name="rotate",
    )(*(pltpu.with_memory_space_constraint(x, pltpu.HBM) for x in (psi, rotation, acc)))
    out = pl.pallas_call(
        functools.partial(finish, n_bands),
        out_shape=jax.ShapeDtypeStruct((nb, mrows), jnp.float32),
        in_specs=[vmem] * 3,
        out_specs=hbm,
        scratch_shapes=[
            pltpu.VMEM((nb // tall, tall, mrows), jnp.float32),
            pltpu.SemaphoreType.DMA((nb // tall,)),
        ],
        compiler_params=pltpu.CompilerParams(vmem_limit_bytes=24 * mib),
        cost_estimate=pl.CostEstimate(
            flops=8 * nb * mrows * kz, bytes_accessed=4 * nb * mrows, transcendentals=0),
        name="finish",
    )(*(pltpu.with_memory_space_constraint(x, pltpu.VMEM) for x in partial))
    return out.T


def solution(mesh):
    sizes = mesh.shape["rows"], mesh.shape["bands"]
    specs = P("rows", "bands")
    return jax.shard_map(
        functools.partial(local, *sizes), mesh=mesh, in_specs=(specs,) * 3, out_specs=specs, check_vma=False)
```

```python
import functools

import jax
import jax.numpy as jnp
from jax import lax
from jax.experimental import pallas as pl
from jax.experimental.pallas import tpu as pltpu
from jax.sharding import PartitionSpec as P

MESH = pl.DeviceIdType.MESH
CHUNK = 256


def split(x):
    high = x.astype(jnp.bfloat16)
    low = (x - high.astype(jnp.float32)).astype(jnp.bfloat16)
    return high, low


def block_rows(nb):
    fit = [rows for rows in range(16, 513, 16) if nb % rows == 0]
    return max(fit, default=nb)


def rot_operand(block):
    high = block.astype(jnp.bfloat16).astype(jnp.float32)
    both = jnp.concatenate([high, block - high], axis=0).T.astype(jnp.bfloat16)
    return jnp.concatenate([both, both], axis=1)


def psi_operand(block):
    high, low = split(block)
    return jnp.concatenate([high, high, low, low], axis=0)


def parts_of(n_rows):
    return 2 if n_rows == 8 else 1


def kernel(n_rows, n_bands, psi_ref, rot_ref, acc_ref, out_ref, rot_op, psi_late,
           psi_all, rot_all, psi_early,
           psi_recv, psi_send, rot_recv, peer_send, twin_send, local_sem):
    r = lax.axis_index("rows")
    z = lax.axis_index("bands")
    n_chips = n_rows // 2
    chip, core = r // 2, r % 2
    twin = 2 * chip + 1 - core
    kz, mrows = psi_ref.shape
    kr, nb = rot_ref.shape
    chunks = mrows // CHUNK
    square = n_chips == 4
    parts = parts_of(n_rows)
    x, y = chip % 2, chip // 2
    xn = 2 * (2 * y + 1 - x) + core
    yn = 2 * (2 * (1 - y) + x) + core
    dn = 2 * (2 * (1 - y) + 1 - x) + core

    def peer(d):
        return 2 * lax.rem(chip + d, n_chips) + core

    def columns(c):
        return pl.ds(pl.multiple_of(c * CHUNK, CHUNK), CHUNK)

    load_acc = pltpu.make_async_copy(acc_ref, out_ref, local_sem.at[0])
    load_psi = pltpu.make_async_copy(psi_ref, psi_all.at[z], local_sem.at[1])
    load_rot = pltpu.make_async_copy(rot_ref, rot_all.at[r], local_sem.at[2])

    barrier = pltpu.get_barrier_semaphore()

    def greet(rows, bands):
        pl.semaphore_signal(barrier, inc=1, device_id=(rows, bands), device_id_type=MESH)

    pl.when(z > 0)(lambda: greet(r, z - 1))
    pl.when(z < n_bands - 1)(lambda: greet(r, z + 1))
    greet(twin, z)

    @pl.loop(1, n_chips)
    def _(d):
        greet(peer(d), z)

    expected = n_chips + jnp.where(z > 0, 1, 0) + jnp.where(z < n_bands - 1, 1, 0)
    pl.semaphore_wait(barrier, expected)

    def psi_copy(source, c, way, own=False):
        here = psi_ref if own else psi_all.at[source]
        target = z + 2 * way - 1
        return pltpu.make_async_remote_copy(
            src_ref=here.at[:, columns(c)],
            dst_ref=psi_all.at[source, :, columns(c)],
            send_sem=psi_send.at[way, source, c],
            recv_sem=psi_recv.at[source, c],
            device_id=(r, target), device_id_type=MESH)

    def rot_copy(source, part, target, send_sem, own=False):
        here = rot_ref if own else rot_all.at[source]
        rows = pl.ds(part * (kr // parts), kr // parts)
        return pltpu.make_async_remote_copy(
            src_ref=here.at[rows],
            dst_ref=rot_all.at[source, rows],
            send_sem=send_sem, recv_sem=rot_recv.at[source, part],
            device_id=(target, z), device_id_type=MESH)

    def own_psi(c):
        pl.when(z > 0)(lambda: psi_copy(z, c, 0, own=True).start())
        pl.when(z < n_bands - 1)(lambda: psi_copy(z, c, 1, own=True).start())

    def own_psi_sent(c):
        pl.when(z > 0)(lambda: psi_copy(z, c, 0, own=True).wait_send())
        pl.when(z < n_bands - 1)(lambda: psi_copy(z, c, 1, own=True).wait_send())

    def pass_on(h, c):
        @pl.when((z - h >= 0) & (z + 1 < n_bands))
        def _():
            copy = psi_copy(z - h, c, 1)
            copy.wait_recv()
            copy.start()

        @pl.when((z + h < n_bands) & (z > 0))
        def _():
            copy = psi_copy(z + h, c, 0)
            copy.wait_recv()
            copy.start()

    def to_twin(source, part, d, wait=True):
        copy = rot_copy(source, part, twin, twin_send.at[d, part], own=not wait)
        if wait:
            copy.wait_recv()
        copy.start()

    for c in range(min(2, chunks)):
        own_psi(c)

    if square:
        sends = [(xn, 0, 1), (yn, 1, 2), (xn, 1, 1), (yn, 0, 2)]
        for target, part, d in sends:
            rot_copy(r, part, target, peer_send.at[d, part], own=True).start()
    else:
        @pl.loop(1, n_chips)
        def _(d):
            rot_copy(r, 0, peer(d), peer_send.at[d, 0], own=True).start()
    for part in range(parts):
        to_twin(r, part, 0, wait=False)
    load_psi.start()
    load_rot.start()
    load_acc.start()

    @pl.loop(2, chunks)
    def _(c):
        own_psi_sent(c - 2)
        own_psi(c)

    def make_operand(s):
        def columns_from(start, width):
            here = pl.ds(start, width)
            block = rot_all[pl.ds(2 * s, 2), :, here].reshape(kz, width)
            rot_op[s, here, :] = rot_operand(block)

        full = nb // 128
        group = 5 if full % 5 == 0 else 1

        @pl.loop(0, full // group)
        def _(i):
            for j in range(group):
                columns_from(pl.multiple_of((i * group + j) * 128, 128), 128)

        if nb % 128:
            columns_from(full * 128, nb % 128)

    def from_twin(s):
        for part in range(parts):
            rot_copy(2 * s + 1 - core, part, twin, twin_send.at[0, part]).wait_recv()

    load_rot.wait()
    from_twin(chip)
    make_operand(chip)

    last_hop = n_bands - 2
    if n_bands > 3:
        for c in range(min(2, chunks)):
            pass_on(1, c)
    if square:
        for source, part, target, d in ((xn, 0, yn, 1), (yn, 1, xn, 2)):
            to_twin(source, part, d)
            rot_copy(source, part, target, peer_send.at[0, part]).start()
    if n_bands > 3:
        for c in range(2, chunks):
            pass_on(1, c)

        @pl.loop(2, last_hop)
        def _(h):
            pl.loop(0, chunks)(lambda c: pass_on(h, c))

    if square:
        to_twin(xn, 1, 1)
        to_twin(yn, 0, 2)
        for s in (xn // 2, yn // 2):
            from_twin(s)
            make_operand(s)
        if n_bands > 2:
            for c in range(min(2, chunks)):
                pass_on(last_hop, c)
        for part in range(parts):
            to_twin(dn, part, 3)
        from_twin(dn // 2)
        make_operand(dn // 2)
    else:
        @pl.loop(1, n_chips)
        def _(d):
            to_twin(peer(n_chips - d), 0, d)

        if n_bands > 2:
            for c in range(min(2, chunks)):
                pass_on(last_hop, c)

        @pl.loop(1, n_chips)
        def _(d):
            s = lax.rem(chip + d, n_chips)
            from_twin(s)
            make_operand(s)

    far_down = 2 * z >= n_bands
    late = jnp.where(far_down, 0, n_bands - 2)
    first = jnp.where(far_down, 2, 0)
    inward = jnp.where(far_down, 0, 1)
    at_end = (z == 0) | (z == n_bands - 1)

    load_psi.wait()

    @pl.when(at_end)
    def _():
        @pl.loop(1, n_bands - 2)
        def _(j):
            source = j + first // 2
            pl.loop(0, chunks)(lambda c: psi_copy(source, c, inward).wait_recv())

    @pl.loop(0, n_bands - 2)
    def _(j):
        psi_early[j] = psi_operand(psi_all[first + j])

    load_acc.wait()
    tall = block_rows(nb)
    blocks = nb // tall

    @pl.loop(0, blocks)
    def _(block):
        if n_bands > 2:
            pl.when(block + 2 < chunks)(lambda: pass_on(last_hop, block + 2))
        rows = pl.ds(pl.multiple_of(block * tall, tall), tall)
        left = jnp.concatenate([rot_op[first + j, rows, :] for j in range(n_bands - 2)], axis=1)
        out_ref[rows, :] += jnp.dot(
            left, psi_early[...].reshape(-1, mrows), preferred_element_type=jnp.float32)

    if n_bands > 2:
        for c in range(2 + blocks, chunks):
            pass_on(last_hop, c)

    for j in range(2):
        @pl.when(at_end)
        def _():
            pl.loop(0, chunks)(lambda c: psi_copy(late + j, c, inward).wait_recv())

        psi_late[j] = psi_operand(psi_all[late + j])

    pl.loop(max(0, chunks - 2), chunks)(own_psi_sent)

    @pl.loop(0, chunks)
    def _(c):
        @pl.when(z < n_bands - 1)
        def _():
            @pl.loop(0, z)
            def _(source):
                psi_copy(source, c, 1).wait_send()

        @pl.when(z > 0)
        def _():
            @pl.loop(z + 1, n_bands)
            def _(source):
                psi_copy(source, c, 0).wait_send()

    if square:
        for target, part, d in sends + [(yn, 0, 0), (xn, 1, 0)]:
            rot_copy(r, part, target, peer_send.at[d, part]).wait_send()
    else:
        @pl.loop(1, n_chips)
        def _(d):
            rot_copy(r, 0, peer(d), peer_send.at[d, 0]).wait_send()

    @pl.loop(0, n_chips)
    def _(d):
        for part in range(parts):
            rot_copy(r, part, twin, twin_send.at[d, part]).wait_send()


def finish(n_bands, sum_ref, rot_ref, psi_ref, out_ref, held, sems):
    blocks, tall, _ = held.shape
    late = jnp.where(2 * lax.axis_index("bands") >= n_bands, 0, n_bands - 2)

    def write(block):
        rows = pl.ds(pl.multiple_of(block * tall, tall), tall)
        return pltpu.make_async_copy(held.at[block], out_ref.at[rows], sems.at[block])

    @pl.loop(0, blocks)
    def _(block):
        rows = pl.ds(pl.multiple_of(block * tall, tall), tall)
        left = jnp.concatenate([rot_ref[late, rows, :], rot_ref[late + 1, rows, :]], axis=1)
        right = psi_ref[...].reshape(-1, psi_ref.shape[2])
        held[block] = sum_ref[rows, :] + jnp.dot(left, right, preferred_element_type=jnp.float32)
        write(block).start()

    pl.loop(0, blocks)(lambda block: write(block).wait())


def local(n_rows, n_bands, psi_panels, rotation, accumulated):
    psi, acc = psi_panels.T, accumulated.T
    kz, mrows = psi.shape
    kr, nb = rotation.shape
    chunks = mrows // CHUNK
    parts = parts_of(n_rows)
    tall = block_rows(nb)
    vmem, hbm = pl.BlockSpec(memory_space=pltpu.VMEM), pl.BlockSpec(memory_space=pltpu.HBM)
    mib = 1024 * 1024
    partial = pl.pallas_call(
        functools.partial(kernel, n_rows, n_bands),
        out_shape=[
            pltpu.VMEM((nb, mrows), jnp.float32),
            pltpu.VMEM((n_bands, nb, 4 * kz), jnp.bfloat16),
            pltpu.VMEM((2, 4 * kz, mrows), jnp.bfloat16),
        ],
        in_specs=[hbm] * 3,
        out_specs=[vmem] * 3,
        scratch_shapes=[
            pltpu.VMEM((n_bands, kz, mrows), jnp.float32),
            pltpu.VMEM((n_rows, kr, nb), jnp.float32),
            pltpu.VMEM((n_bands - 2, 4 * kz, mrows), jnp.bfloat16),
            pltpu.SemaphoreType.DMA((n_bands, chunks)),
            pltpu.SemaphoreType.DMA((2, n_bands, chunks)),
            pltpu.SemaphoreType.DMA((n_rows, parts)),
            pltpu.SemaphoreType.DMA((n_rows // 2, parts)),
            pltpu.SemaphoreType.DMA((n_rows // 2, parts)),
            pltpu.SemaphoreType.DMA((3,)),
        ],
        compiler_params=pltpu.CompilerParams(
            collective_id=0, has_side_effects=True, vmem_limit_bytes=24 * mib),
        cost_estimate=pl.CostEstimate(
            flops=6 * nb * mrows * n_rows * kr, bytes_accessed=4 * nb * mrows, transcendentals=0),
        name="rotate",
    )(*(pltpu.with_memory_space_constraint(x, pltpu.HBM) for x in (psi, rotation, acc)))
    out = pl.pallas_call(
        functools.partial(finish, n_bands),
        out_shape=jax.ShapeDtypeStruct((nb, mrows), jnp.float32),
        in_specs=[vmem] * 3,
        out_specs=hbm,
        scratch_shapes=[
            pltpu.VMEM((nb // tall, tall, mrows), jnp.float32),
            pltpu.SemaphoreType.DMA((nb // tall,)),
        ],
        compiler_params=pltpu.CompilerParams(vmem_limit_bytes=24 * mib),
        cost_estimate=pl.CostEstimate(
            flops=16 * nb * mrows * kz, bytes_accessed=4 * nb * mrows, transcendentals=0),
        name="finish",
    )(*(pltpu.with_memory_space_constraint(x, pltpu.VMEM) for x in partial))
    return out.T


def solution(mesh):
    sizes = mesh.shape["rows"], mesh.shape["bands"]
    specs = P("rows", "bands")
    return jax.shard_map(
        functools.partial(local, *sizes), mesh=mesh, in_specs=(specs,) * 3, out_specs=specs, check_vma=False)
```

```python
import functools

import jax
import jax.numpy as jnp
from jax import lax
from jax.experimental import pallas as pl
from jax.experimental.pallas import tpu as pltpu
from jax.sharding import PartitionSpec as P

MESH = pl.DeviceIdType.MESH
CHUNK = 256


def split(x):
    high = x.astype(jnp.bfloat16)
    low = (x - high.astype(jnp.float32)).astype(jnp.bfloat16)
    return high, low


def block_rows(nb):
    fit = [rows for rows in range(16, 513, 16) if nb % rows == 0]
    return max(fit, default=nb)


def rot_operand(block):
    high = block.astype(jnp.bfloat16).astype(jnp.float32)
    both = jnp.concatenate([high, block - high], axis=0).T.astype(jnp.bfloat16)
    return jnp.concatenate([both, both], axis=1)


def psi_operand(block):
    high, low = split(block)
    return jnp.concatenate([high, high, low, low], axis=0)


def parts_of(n_rows):
    return 2 if n_rows == 8 else 1


def kernel(n_rows, n_bands, psi_ref, rot_ref, acc_ref, out_ref, rot_op, psi_late,
           psi_all, rot_all, psi_early,
           psi_recv, psi_send, rot_recv, peer_send, twin_send, local_sem):
    r = lax.axis_index("rows")
    z = lax.axis_index("bands")
    n_chips = n_rows // 2
    chip, core = r // 2, r % 2
    twin = 2 * chip + 1 - core
    kz, mrows = psi_ref.shape
    kr, nb = rot_ref.shape
    chunks = mrows // CHUNK
    square = n_chips == 4
    parts = parts_of(n_rows)
    x, y = chip % 2, chip // 2
    xn = 2 * (2 * y + 1 - x) + core
    yn = 2 * (2 * (1 - y) + x) + core
    dn = 2 * (2 * (1 - y) + 1 - x) + core

    def peer(d):
        return 2 * lax.rem(chip + d, n_chips) + core

    def columns(c):
        return pl.ds(pl.multiple_of(c * CHUNK, CHUNK), CHUNK)

    load_acc = pltpu.make_async_copy(acc_ref, out_ref, local_sem.at[0])
    load_psi = pltpu.make_async_copy(psi_ref, psi_all.at[z], local_sem.at[1])
    load_rot = pltpu.make_async_copy(rot_ref, rot_all.at[r], local_sem.at[2])

    barrier = pltpu.get_barrier_semaphore()

    def greet(rows, bands):
        pl.semaphore_signal(barrier, inc=1, device_id=(rows, bands), device_id_type=MESH)

    pl.when(z > 0)(lambda: greet(r, z - 1))
    pl.when(z < n_bands - 1)(lambda: greet(r, z + 1))
    greet(twin, z)

    @pl.loop(1, n_chips)
    def _(d):
        greet(peer(d), z)

    expected = n_chips + jnp.where(z > 0, 1, 0) + jnp.where(z < n_bands - 1, 1, 0)
    pl.semaphore_wait(barrier, expected)

    def psi_copy(source, c, way, own=False):
        here = psi_ref if own else psi_all.at[source]
        target = z + 2 * way - 1
        return pltpu.make_async_remote_copy(
            src_ref=here.at[:, columns(c)],
            dst_ref=psi_all.at[source, :, columns(c)],
            send_sem=psi_send.at[way, source, c],
            recv_sem=psi_recv.at[source, c],
            device_id=(r, target), device_id_type=MESH)

    def rot_copy(source, part, target, send_sem, own=False):
        here = rot_ref if own else rot_all.at[source]
        rows = pl.ds(part * (kr // parts), kr // parts)
        return pltpu.make_async_remote_copy(
            src_ref=here.at[rows],
            dst_ref=rot_all.at[source, rows],
            send_sem=send_sem, recv_sem=rot_recv.at[source, part],
            device_id=(target, z), device_id_type=MESH)

    def own_psi(c):
        pl.when(z > 0)(lambda: psi_copy(z, c, 0, own=True).start())
        pl.when(z < n_bands - 1)(lambda: psi_copy(z, c, 1, own=True).start())

    def own_psi_sent(c):
        pl.when(z > 0)(lambda: psi_copy(z, c, 0, own=True).wait_send())
        pl.when(z < n_bands - 1)(lambda: psi_copy(z, c, 1, own=True).wait_send())

    def pass_on(h, c):
        @pl.when((z - h >= 0) & (z + 1 < n_bands))
        def _():
            copy = psi_copy(z - h, c, 1)
            copy.wait_recv()
            copy.start()

        @pl.when((z + h < n_bands) & (z > 0))
        def _():
            copy = psi_copy(z + h, c, 0)
            copy.wait_recv()
            copy.start()

    def to_twin(source, part, d, wait=True):
        copy = rot_copy(source, part, twin, twin_send.at[d, part], own=not wait)
        if wait:
            copy.wait_recv()
        copy.start()

    for c in range(min(2, chunks)):
        own_psi(c)

    if square:
        sends = [(xn, 0, 1), (yn, 1, 2), (xn, 1, 1), (yn, 0, 2)]
        for target, part, d in sends:
            rot_copy(r, part, target, peer_send.at[d, part], own=True).start()
    else:
        @pl.loop(1, n_chips)
        def _(d):
            rot_copy(r, 0, peer(d), peer_send.at[d, 0], own=True).start()
    for part in range(parts):
        to_twin(r, part, 0, wait=False)
    load_psi.start()
    load_rot.start()
    load_acc.start()

    @pl.loop(2, chunks)
    def _(c):
        own_psi_sent(c - 2)
        own_psi(c)

    def make_operand(s):
        def columns_from(start, width):
            here = pl.ds(start, width)
            block = rot_all[pl.ds(2 * s, 2), :, here].reshape(kz, width)
            rot_op[s, here, :] = rot_operand(block)

        full = nb // 128
        group = 5 if full % 5 == 0 else 1

        @pl.loop(0, full // group)
        def _(i):
            for j in range(group):
                columns_from(pl.multiple_of((i * group + j) * 128, 128), 128)

        if nb % 128:
            columns_from(full * 128, nb % 128)

    def from_twin(s):
        for part in range(parts):
            rot_copy(2 * s + 1 - core, part, twin, twin_send.at[0, part]).wait_recv()

    load_rot.wait()
    from_twin(chip)
    make_operand(chip)

    last_hop = n_bands - 2
    if n_bands > 3:
        for c in range(min(2, chunks)):
            pass_on(1, c)
    if square:
        for source, part, target, d in ((xn, 0, yn, 1), (yn, 1, xn, 2)):
            to_twin(source, part, d)
            rot_copy(source, part, target, peer_send.at[0, part]).start()
    if n_bands > 3:
        for c in range(2, chunks):
            pass_on(1, c)

        @pl.loop(2, last_hop)
        def _(h):
            pl.loop(0, chunks)(lambda c: pass_on(h, c))

    if square:
        to_twin(xn, 1, 1)
        to_twin(yn, 0, 2)
        for s in (xn // 2, yn // 2):
            from_twin(s)
            make_operand(s)
        if n_bands > 2:
            for c in range(min(2, chunks)):
                pass_on(last_hop, c)
        for part in range(parts):
            to_twin(dn, part, 3)
        from_twin(dn // 2)
        make_operand(dn // 2)
    else:
        @pl.loop(1, n_chips)
        def _(d):
            to_twin(peer(n_chips - d), 0, d)

        if n_bands > 2:
            for c in range(min(2, chunks)):
                pass_on(last_hop, c)

        @pl.loop(1, n_chips)
        def _(d):
            s = lax.rem(chip + d, n_chips)
            from_twin(s)
            make_operand(s)

    far_down = 2 * z >= n_bands
    late = jnp.where(far_down, 0, n_bands - 1)
    first = jnp.where(far_down, 1, 0)
    inward = jnp.where(far_down, 0, 1)
    at_end = (z == 0) | (z == n_bands - 1)

    load_psi.wait()

    @pl.when(at_end)
    def _():
        @pl.loop(1, n_bands - 1)
        def _(source):
            pl.loop(0, chunks)(lambda c: psi_copy(source, c, inward).wait_recv())

    @pl.loop(0, n_bands - 1)
    def _(j):
        psi_early[j] = psi_operand(psi_all[first + j])

    load_acc.wait()
    tall = block_rows(nb)
    blocks = nb // tall

    @pl.loop(0, blocks)
    def _(block):
        if n_bands > 2:
            pl.when(block + 2 < chunks)(lambda: pass_on(last_hop, block + 2))
        rows = pl.ds(pl.multiple_of(block * tall, tall), tall)
        left = jnp.concatenate([rot_op[first + j, rows, :] for j in range(n_bands - 1)], axis=1)
        out_ref[rows, :] += jnp.dot(
            left, psi_early[...].reshape(-1, mrows), preferred_element_type=jnp.float32)

    if n_bands > 2:
        for c in range(2 + blocks, chunks):
            pass_on(last_hop, c)

    @pl.loop(0, chunks)
    def _(c):
        pl.when(at_end)(lambda: psi_copy(late, c, inward).wait_recv())
        psi_late[:, columns(c)] = psi_operand(psi_all[late, :, columns(c)])

    pl.loop(max(0, chunks - 2), chunks)(own_psi_sent)

    @pl.loop(0, chunks)
    def _(c):
        @pl.when(z < n_bands - 1)
        def _():
            @pl.loop(0, z)
            def _(source):
                psi_copy(source, c, 1).wait_send()

        @pl.when(z > 0)
        def _():
            @pl.loop(z + 1, n_bands)
            def _(source):
                psi_copy(source, c, 0).wait_send()

    if square:
        for target, part, d in sends + [(yn, 0, 0), (xn, 1, 0)]:
            rot_copy(r, part, target, peer_send.at[d, part]).wait_send()
    else:
        @pl.loop(1, n_chips)
        def _(d):
            rot_copy(r, 0, peer(d), peer_send.at[d, 0]).wait_send()

    @pl.loop(0, n_chips)
    def _(d):
        for part in range(parts):
            rot_copy(r, part, twin, twin_send.at[d, part]).wait_send()


def finish(n_bands, tall, sum_ref, rot_ref, psi_ref, out_ref, held, sems):
    late = jnp.where(2 * lax.axis_index("bands") >= n_bands, 0, n_bands - 1)
    blocks = held.shape[0] // tall
    lead = [(0, tall // 5), (tall // 5, tall * 2 // 5), (tall * 3 // 5, tall * 2 // 5)]
    if tall % 80:
        lead = [(0, tall)]

    def write(rows, i):
        return pltpu.make_async_copy(held.at[rows], out_ref.at[rows], sems.at[i])

    def add(rows, i):
        held[rows, :] = sum_ref[rows, :] + jnp.dot(
            rot_ref[late, rows, :], psi_ref[...], preferred_element_type=jnp.float32)
        write(rows, i).start()

    def block_at(block):
        return pl.ds(pl.multiple_of(block * tall, tall), tall)

    for i, (start, size) in enumerate(lead):
        add(pl.ds(start, size), i)
    pl.loop(1, blocks)(lambda block: add(block_at(block), block + 2))
    for i, (start, size) in enumerate(lead):
        write(pl.ds(start, size), i).wait()
    pl.loop(1, blocks)(lambda block: write(block_at(block), block + 2).wait())


def local(n_rows, n_bands, psi_panels, rotation, accumulated):
    psi, acc = psi_panels.T, accumulated.T
    kz, mrows = psi.shape
    kr, nb = rotation.shape
    chunks = mrows // CHUNK
    parts = parts_of(n_rows)
    tall = block_rows(nb)
    vmem, hbm = pl.BlockSpec(memory_space=pltpu.VMEM), pl.BlockSpec(memory_space=pltpu.HBM)
    mib = 1024 * 1024
    partial = pl.pallas_call(
        functools.partial(kernel, n_rows, n_bands),
        out_shape=[
            pltpu.VMEM((nb, mrows), jnp.float32),
            pltpu.VMEM((n_bands, nb, 4 * kz), jnp.bfloat16),
            pltpu.VMEM((4 * kz, mrows), jnp.bfloat16),
        ],
        in_specs=[hbm] * 3,
        out_specs=[vmem] * 3,
        scratch_shapes=[
            pltpu.VMEM((n_bands, kz, mrows), jnp.float32),
            pltpu.VMEM((n_rows, kr, nb), jnp.float32),
            pltpu.VMEM((n_bands - 1, 4 * kz, mrows), jnp.bfloat16),
            pltpu.SemaphoreType.DMA((n_bands, chunks)),
            pltpu.SemaphoreType.DMA((2, n_bands, chunks)),
            pltpu.SemaphoreType.DMA((n_rows, parts)),
            pltpu.SemaphoreType.DMA((n_rows // 2, parts)),
            pltpu.SemaphoreType.DMA((n_rows // 2, parts)),
            pltpu.SemaphoreType.DMA((3,)),
        ],
        compiler_params=pltpu.CompilerParams(
            collective_id=0, has_side_effects=True, vmem_limit_bytes=24 * mib),
        cost_estimate=pl.CostEstimate(
            flops=6 * nb * mrows * n_rows * kr, bytes_accessed=4 * nb * mrows, transcendentals=0),
        name="rotate",
    )(*(pltpu.with_memory_space_constraint(x, pltpu.HBM) for x in (psi, rotation, acc)))
    out = pl.pallas_call(
        functools.partial(finish, n_bands, tall),
        out_shape=jax.ShapeDtypeStruct((nb, mrows), jnp.float32),
        in_specs=[vmem] * 3,
        out_specs=hbm,
        scratch_shapes=[
            pltpu.VMEM((nb, mrows), jnp.float32),
            pltpu.SemaphoreType.DMA((nb // tall + 2,)),
        ],
        compiler_params=pltpu.CompilerParams(vmem_limit_bytes=24 * mib),
        cost_estimate=pl.CostEstimate(
            flops=8 * nb * mrows * kz, bytes_accessed=4 * nb * mrows, transcendentals=0),
        name="finish",
    )(*(pltpu.with_memory_space_constraint(x, pltpu.VMEM) for x in partial))
    return out.T


def solution(mesh):
    sizes = mesh.shape["rows"], mesh.shape["bands"]
    specs = P("rows", "bands")
    return jax.shard_map(
        functools.partial(local, *sizes), mesh=mesh, in_specs=(specs,) * 3, out_specs=specs, check_vma=False)
```

```python
import functools

import jax
import jax.numpy as jnp
from jax import lax
from jax.experimental import pallas as pl
from jax.experimental.pallas import tpu as pltpu
from jax.sharding import PartitionSpec as P

MESH = pl.DeviceIdType.MESH


def split(x):
    high = x.astype(jnp.bfloat16)
    low = (x - high.astype(jnp.float32)).astype(jnp.bfloat16)
    return high, low


def chunks_of(kz):
    return max(n for n in (1, 2, 4) if kz % (8 * n) == 0)


def block_rows(nb):
    fit = [rows for rows in range(16, 513, 16) if nb % rows == 0]
    return max(fit, default=nb)


def rot_operand(block):
    high = block.astype(jnp.bfloat16).astype(jnp.float32)
    both = jnp.concatenate([high, block - high], axis=0).T.astype(jnp.bfloat16)
    return jnp.concatenate([both, both], axis=1)


def psi_operand(block):
    high, low = split(block)
    return jnp.concatenate([high, high, low, low], axis=0)


def parts_of(n_rows):
    return 2 if n_rows == 8 else 1


def kernel(n_rows, n_bands, psi_ref, rot_ref, acc_ref, out_ref, rot_op, psi_late,
           psi_all, rot_all, psi_early,
           psi_recv, psi_send, rot_recv, peer_send, twin_send, local_sem):
    r = lax.axis_index("rows")
    z = lax.axis_index("bands")
    n_chips = n_rows // 2
    chip, core = r // 2, r % 2
    twin = 2 * chip + 1 - core
    kz, mrows = psi_ref.shape
    kr, nb = rot_ref.shape
    chunks = chunks_of(kz)
    square = n_chips == 4
    parts = parts_of(n_rows)
    x, y = chip % 2, chip // 2
    xn = 2 * (2 * y + 1 - x) + core
    yn = 2 * (2 * (1 - y) + x) + core
    dn = 2 * (2 * (1 - y) + 1 - x) + core

    def peer(d):
        return 2 * lax.rem(chip + d, n_chips) + core

    def panel_rows(c):
        return pl.ds(pl.multiple_of(c * (kz // chunks), kz // chunks), kz // chunks)

    load_acc = pltpu.make_async_copy(acc_ref, out_ref, local_sem.at[0])
    load_psi = pltpu.make_async_copy(psi_ref, psi_all.at[z], local_sem.at[1])
    load_rot = pltpu.make_async_copy(rot_ref, rot_all.at[r], local_sem.at[2])

    barrier = pltpu.get_barrier_semaphore()

    def greet(rows, bands):
        pl.semaphore_signal(barrier, inc=1, device_id=(rows, bands), device_id_type=MESH)

    pl.when(z > 0)(lambda: greet(r, z - 1))
    pl.when(z < n_bands - 1)(lambda: greet(r, z + 1))
    greet(twin, z)

    @pl.loop(1, n_chips)
    def _(d):
        greet(peer(d), z)

    expected = n_chips + jnp.where(z > 0, 1, 0) + jnp.where(z < n_bands - 1, 1, 0)
    pl.semaphore_wait(barrier, expected)

    def psi_copy(source, c, way, own=False):
        here = psi_ref if own else psi_all.at[source]
        target = z + 2 * way - 1
        return pltpu.make_async_remote_copy(
            src_ref=here.at[panel_rows(c)],
            dst_ref=psi_all.at[source, panel_rows(c)],
            send_sem=psi_send.at[way, source, c],
            recv_sem=psi_recv.at[source, c],
            device_id=(r, target), device_id_type=MESH)

    def rot_copy(source, part, target, send_sem, own=False):
        here = rot_ref if own else rot_all.at[source]
        rows = pl.ds(part * (kr // parts), kr // parts)
        return pltpu.make_async_remote_copy(
            src_ref=here.at[rows],
            dst_ref=rot_all.at[source, rows],
            send_sem=send_sem, recv_sem=rot_recv.at[source, part],
            device_id=(target, z), device_id_type=MESH)

    def own_psi(c):
        pl.when(z > 0)(lambda: psi_copy(z, c, 0, own=True).start())
        pl.when(z < n_bands - 1)(lambda: psi_copy(z, c, 1, own=True).start())

    def own_psi_sent(c):
        pl.when(z > 0)(lambda: psi_copy(z, c, 0, own=True).wait_send())
        pl.when(z < n_bands - 1)(lambda: psi_copy(z, c, 1, own=True).wait_send())

    def pass_on(h, c):
        @pl.when((z - h >= 0) & (z + 1 < n_bands))
        def _():
            copy = psi_copy(z - h, c, 1)
            copy.wait_recv()
            copy.start()

        @pl.when((z + h < n_bands) & (z > 0))
        def _():
            copy = psi_copy(z + h, c, 0)
            copy.wait_recv()
            copy.start()

    def to_twin(source, part, d, wait=True):
        copy = rot_copy(source, part, twin, twin_send.at[d, part], own=not wait)
        if wait:
            copy.wait_recv()
        copy.start()

    for c in range(min(2, chunks)):
        own_psi(c)

    if square:
        sends = [(xn, 0, 1), (yn, 1, 2), (xn, 1, 1), (yn, 0, 2)]
        for target, part, d in sends:
            rot_copy(r, part, target, peer_send.at[d, part], own=True).start()
    else:
        @pl.loop(1, n_chips)
        def _(d):
            rot_copy(r, 0, peer(d), peer_send.at[d, 0], own=True).start()
    for part in range(parts):
        to_twin(r, part, 0, wait=False)
    load_psi.start()
    load_rot.start()
    load_acc.start()

    @pl.loop(2, chunks)
    def _(c):
        own_psi_sent(c - 2)
        own_psi(c)

    def make_operand(s):
        def columns_from(start, width):
            here = pl.ds(start, width)
            block = rot_all[pl.ds(2 * s, 2), :, here].reshape(kz, width)
            rot_op[s, here, :] = rot_operand(block)

        full = nb // 128
        group = 5 if full % 5 == 0 else 1

        @pl.loop(0, full // group)
        def _(i):
            for j in range(group):
                columns_from(pl.multiple_of((i * group + j) * 128, 128), 128)

        if nb % 128:
            columns_from(full * 128, nb % 128)

    def from_twin(s):
        for part in range(parts):
            rot_copy(2 * s + 1 - core, part, twin, twin_send.at[0, part]).wait_recv()

    load_rot.wait()
    from_twin(chip)
    make_operand(chip)

    last_hop = n_bands - 2
    if n_bands > 3:
        for c in range(min(2, chunks)):
            pass_on(1, c)
    if square:
        for source, part, target, d in ((xn, 0, yn, 1), (yn, 1, xn, 2)):
            to_twin(source, part, d)
            rot_copy(source, part, target, peer_send.at[0, part]).start()
    if n_bands > 3:
        for c in range(2, chunks):
            pass_on(1, c)

        @pl.loop(2, last_hop)
        def _(h):
            pl.loop(0, chunks)(lambda c: pass_on(h, c))

    if square:
        to_twin(xn, 1, 1)
        to_twin(yn, 0, 2)
        for s in (xn // 2, yn // 2):
            from_twin(s)
            make_operand(s)
        if n_bands > 2:
            for c in range(min(2, chunks)):
                pass_on(last_hop, c)
        for part in range(parts):
            to_twin(dn, part, 3)
        from_twin(dn // 2)
        make_operand(dn // 2)
    else:
        @pl.loop(1, n_chips)
        def _(d):
            to_twin(peer(n_chips - d), 0, d)

        if n_bands > 2:
            for c in range(min(2, chunks)):
                pass_on(last_hop, c)

        @pl.loop(1, n_chips)
        def _(d):
            s = lax.rem(chip + d, n_chips)
            from_twin(s)
            make_operand(s)

    far_down = 2 * z >= n_bands
    late = jnp.where(far_down, 0, n_bands - 1)
    first = jnp.where(far_down, 1, 0)
    inward = jnp.where(far_down, 0, 1)
    at_end = (z == 0) | (z == n_bands - 1)

    load_psi.wait()

    @pl.when(at_end)
    def _():
        @pl.loop(1, n_bands - 1)
        def _(source):
            pl.loop(0, chunks)(lambda c: psi_copy(source, c, inward).wait_recv())

    @pl.loop(0, n_bands - 1)
    def _(j):
        psi_early[j] = psi_operand(psi_all[first + j])

    load_acc.wait()
    tall = block_rows(nb)
    blocks = nb // tall

    @pl.loop(0, blocks)
    def _(block):
        if n_bands > 2:
            pl.when(block + 2 < chunks)(lambda: pass_on(last_hop, block + 2))
        rows = pl.ds(pl.multiple_of(block * tall, tall), tall)
        left = jnp.concatenate([rot_op[first + j, rows, :] for j in range(n_bands - 1)], axis=1)
        out_ref[rows, :] += jnp.dot(
            left, psi_early[...].reshape(-1, mrows), preferred_element_type=jnp.float32)

    if n_bands > 2:
        for c in range(2 + blocks, chunks):
            pass_on(last_hop, c)

    @pl.loop(0, chunks)
    def _(c):
        pl.when(at_end)(lambda: psi_copy(late, c, inward).wait_recv())

    psi_late[...] = psi_operand(psi_all[late])

    pl.loop(max(0, chunks - 2), chunks)(own_psi_sent)

    @pl.loop(0, chunks)
    def _(c):
        @pl.when(z < n_bands - 1)
        def _():
            @pl.loop(0, z)
            def _(source):
                psi_copy(source, c, 1).wait_send()

        @pl.when(z > 0)
        def _():
            @pl.loop(z + 1, n_bands)
            def _(source):
                psi_copy(source, c, 0).wait_send()

    if square:
        for target, part, d in sends + [(yn, 0, 0), (xn, 1, 0)]:
            rot_copy(r, part, target, peer_send.at[d, part]).wait_send()
    else:
        @pl.loop(1, n_chips)
        def _(d):
            rot_copy(r, 0, peer(d), peer_send.at[d, 0]).wait_send()

    @pl.loop(0, n_chips)
    def _(d):
        for part in range(parts):
            rot_copy(r, part, twin, twin_send.at[d, part]).wait_send()


def finish(n_bands, tall, sum_ref, rot_ref, psi_ref, out_ref, held, sems):
    late = jnp.where(2 * lax.axis_index("bands") >= n_bands, 0, n_bands - 1)
    blocks = held.shape[0] // tall
    lead = [(0, tall // 5), (tall // 5, tall * 2 // 5), (tall * 3 // 5, tall * 2 // 5)]
    if tall % 80:
        lead = [(0, tall)]

    def write(rows, i):
        return pltpu.make_async_copy(held.at[rows], out_ref.at[rows], sems.at[i])

    def add(rows, i):
        held[rows, :] = sum_ref[rows, :] + jnp.dot(
            rot_ref[late, rows, :], psi_ref[...], preferred_element_type=jnp.float32)
        write(rows, i).start()

    def block_at(block):
        return pl.ds(pl.multiple_of(block * tall, tall), tall)

    for i, (start, size) in enumerate(lead):
        add(pl.ds(start, size), i)
    pl.loop(1, blocks)(lambda block: add(block_at(block), block + 2))
    for i, (start, size) in enumerate(lead):
        write(pl.ds(start, size), i).wait()
    pl.loop(1, blocks)(lambda block: write(block_at(block), block + 2).wait())


def local(n_rows, n_bands, psi_panels, rotation, accumulated):
    psi, acc = psi_panels.T, accumulated.T
    kz, mrows = psi.shape
    kr, nb = rotation.shape
    chunks = chunks_of(kz)
    parts = parts_of(n_rows)
    tall = block_rows(nb)
    vmem, hbm = pl.BlockSpec(memory_space=pltpu.VMEM), pl.BlockSpec(memory_space=pltpu.HBM)
    mib = 1024 * 1024
    partial = pl.pallas_call(
        functools.partial(kernel, n_rows, n_bands),
        out_shape=[
            pltpu.VMEM((nb, mrows), jnp.float32),
            pltpu.VMEM((n_bands, nb, 4 * kz), jnp.bfloat16),
            pltpu.VMEM((4 * kz, mrows), jnp.bfloat16),
        ],
        in_specs=[hbm] * 3,
        out_specs=[vmem] * 3,
        scratch_shapes=[
            pltpu.VMEM((n_bands, kz, mrows), jnp.float32),
            pltpu.VMEM((n_rows, kr, nb), jnp.float32),
            pltpu.VMEM((n_bands - 1, 4 * kz, mrows), jnp.bfloat16),
            pltpu.SemaphoreType.DMA((n_bands, chunks)),
            pltpu.SemaphoreType.DMA((2, n_bands, chunks)),
            pltpu.SemaphoreType.DMA((n_rows, parts)),
            pltpu.SemaphoreType.DMA((n_rows // 2, parts)),
            pltpu.SemaphoreType.DMA((n_rows // 2, parts)),
            pltpu.SemaphoreType.DMA((3,)),
        ],
        compiler_params=pltpu.CompilerParams(
            collective_id=0, has_side_effects=True, vmem_limit_bytes=24 * mib),
        cost_estimate=pl.CostEstimate(
            flops=6 * nb * mrows * n_rows * kr, bytes_accessed=4 * nb * mrows, transcendentals=0),
        name="rotate",
    )(*(pltpu.with_memory_space_constraint(x, pltpu.HBM) for x in (psi, rotation, acc)))
    out = pl.pallas_call(
        functools.partial(finish, n_bands, tall),
        out_shape=jax.ShapeDtypeStruct((nb, mrows), jnp.float32),
        in_specs=[vmem] * 3,
        out_specs=hbm,
        scratch_shapes=[
            pltpu.VMEM((nb, mrows), jnp.float32),
            pltpu.SemaphoreType.DMA((nb // tall + 2,)),
        ],
        compiler_params=pltpu.CompilerParams(vmem_limit_bytes=24 * mib),
        cost_estimate=pl.CostEstimate(
            flops=8 * nb * mrows * kz, bytes_accessed=4 * nb * mrows, transcendentals=0),
        name="finish",
    )(*(pltpu.with_memory_space_constraint(x, pltpu.VMEM) for x in partial))
    return out.T


def solution(mesh):
    sizes = mesh.shape["rows"], mesh.shape["bands"]
    specs = P("rows", "bands")
    return jax.shard_map(
        functools.partial(local, *sizes), mesh=mesh, in_specs=(specs,) * 3, out_specs=specs, check_vma=False)
```
